32 devices in a mesh: seq: 8 (over z, x), head: 4 (over y, core).
Axes of the slice: x: 2, y: 2, z: 4, core: 2. Of those that a mesh axis runs over, the one named last changes fastest.
Arguments:
- queries: bfloat16 [8192, 4096], P('seq', 'head'), may hold values from -6 to 6
- key_rows: bfloat16 [8192, 4096], P('seq', 'head'), may hold values from -6 to 6
- value_rows: bfloat16 [8192, 4096], P('seq', 'head'), may hold values from -6 to 6
- gate_logits: bfloat16 [8192, 4096], P('seq', 'head'), may hold values from -6 to 6
- norm_gain: float32 [4096], P('head'), may hold values from 0.1 to 1.9
- out_weight: bfloat16 [4096, 6144], P('head', 'seq'), may hold values from -0.125 to 0.125
- doc_lengths: int32 [16], replicated, may hold values from 1 to 4096, 8192 in all
Outputs:
- layer_out: bfloat16 [8192, 6144], P('seq', 'head')
The draws below stay inside these ranges and needn't reach their ends.
Inputs may be any that keep to these rules, and one draw needn't show every extreme that they name: `doc_lengths`: the lengths sum to 8192; the longest document has exactly 4096 positions.
All inputs are finite; a program needn't handle non-finite values.
Results may differ from the reference program's by a relative error of at most 0.0057.
Values may be sent and summed in bfloat16 or wider, within the bound.
No kernel may reach another device: no remote copies, remote signals or barrier semaphores. Data moves between devices by JAX's collectives and lax.ppermute only.
A program may use at most 128 MiB of HBM per device.

```python
import math
import jax
import jax.numpy as jnp
import numpy as np
from jax import lax

D = 6144
HEADS = 32
HS = 128
TOK_DEV = 1024
TOKENS = 8192
DOCS = 16
N_SEQ = 8


def strengthened(values, rng, source, target, blocks, factor):
    owner, partner = [(jnp.arange(values.shape[position]) // (values.shape[position] // blocks)).reshape([-1 if axis == position else 1 for axis in range(values.ndim)]) for position in (source, target)]
    chosen = jax.random.permutation(rng, blocks)[partner]
    strong = (owner == chosen) | (owner == (partner + blocks // 2) % blocks)
    return jnp.where(strong, factor * values, values)


def steps_of(rng, dims, shards, low, largest):
    loudness = 1.0
    for position, blocks in shards:
        draws = jax.random.uniform(jax.random.fold_in(jax.random.fold_in(rng, 6), position), (blocks,), jnp.float32, low / len(shards), largest / len(shards))
        loudness = loudness * jnp.repeat(jnp.exp(draws), dims[position] // blocks).reshape((-1,) + (1,) * (len(dims) - 1 - position))
    return loudness


def split_up(number_of, total, most, lean):
    portions = [(1 << 20) // math.isqrt(rank ** lean) + 1 for rank in range(2, number_of + 1)]
    rest, counts = total - most - (number_of - 1), [1] * (number_of - 1)
    while rest > 0:
        free = [i for i in range(number_of - 1) if counts[i] < most]
        whole, remaining = sum([portions[i] for i in free]), rest
        for i in free:
            addition = min(most - counts[i], max(1, remaining * portions[i] // whole), rest)
            counts[i] = counts[i] + addition
            rest = rest - addition
    return np.array([most] + counts)


def ragged_sizes(rng, number_of, total, most, skew):
    if number_of == 2:
        one = jax.random.randint(rng, (), max(1, total - most), min(most, total - 1) + 1)
        return jnp.stack([one, total - one])
    lengths = jnp.asarray(split_up(number_of, total, most, skew), jnp.int32)
    couples = (number_of - 1) // 2
    source_of, receiver = lengths[1:1 + 2 * couples:2], lengths[2:2 + 2 * couples:2]
    slack = jnp.minimum(source_of - 1, most - receiver)
    passed = jax.random.randint(jax.random.fold_in(rng, 1), (couples,), 0, 1 << 20) % (slack + 1)
    lengths = lengths.at[1:1 + 2 * couples:2].set(source_of - passed).at[2:2 + 2 * couples:2].set(receiver + passed)
    return lengths[jax.random.permutation(jax.random.fold_in(rng, 2), number_of)]


def centred(rng, dims, deviation, most, shards=(), kind=jnp.bfloat16):
    gain = steps_of(rng, dims, shards, -0.22, 0.18) if shards else 1.0
    drawn = jax.random.normal(rng, dims, jnp.float32) * deviation * gain
    return jnp.minimum(jnp.maximum(drawn, -most), most).astype(kind)


def gaussian_with(own_key, shape, width, reach, pieces, heavy, held_as=jnp.bfloat16):
    values = width * jax.random.normal(own_key, shape, jnp.float32)
    if pieces:
        values = values * steps_of(own_key, shape, pieces, -0.22, 0.18)
    return jnp.clip(strengthened(values, jax.random.fold_in(own_key, 3), *heavy), -reach, reach).astype(held_as)


def setup_inputs(seed: int = 0) -> dict:
    splits = jax.random.split(jax.random.key(seed), 8)
    return {
        "queries": centred(splits[0], (TOKENS, HEADS * HS), 1.0, 6.0, ((0, 8), (1, 4))),
        "key_rows": centred(splits[1], (TOKENS, HEADS * HS), 1.0, 6.0, ((0, 8), (1, 4))),
        "value_rows": centred(splits[2], (TOKENS, HEADS * HS), 1.0, 6.0, ((0, 8), (1, 4))),
        "gate_logits": centred(splits[3], (TOKENS, HEADS * HS), 1.5, 6.0, ((0, 8), (1, 4))),
        "norm_gain": jnp.clip(1.0 + 0.18 * jax.random.normal(splits[4], (HEADS * HS,), jnp.float32), 0.1, 1.9),
        "out_weight": gaussian_with(splits[5], (HEADS * HS, D), (HEADS * HS) ** -0.5, 0.125, ((0, 4), (1, 8)), (0, 1, 8, 2.0)),
        "doc_lengths": ragged_sizes(splits[6], DOCS, TOKENS, TOKENS // 2, 2).astype(jnp.int32),
    }


norm_eps = 1e-05

def doc_index(doc_lengths, positions):
    starts_all = jnp.cumsum(doc_lengths) - doc_lengths
    hits = (starts_all[None, :] <= positions[:, None]).astype(jnp.int32)
    return lax.optimization_barrier(jnp.sum(hits, axis=1)).astype(jnp.int32) - 1

def reference(queries, key_rows, value_rows, gate_logits, norm_gain, out_weight, doc_lengths):
    positions = jnp.arange(TOKENS, dtype=jnp.int32)
    doc_ids = doc_index(doc_lengths, positions).reshape(N_SEQ, TOK_DEV)
    before_ids = doc_index(doc_lengths, jnp.arange(N_SEQ, dtype=jnp.int32) * TOK_DEV - 1)
    gain_rows = norm_gain.astype(jnp.float32).reshape(HEADS, HS)
    causal = jnp.arange(TOK_DEV)[:, None] >= jnp.arange(TOK_DEV)[None, :]

    def shaped(array):
        return array.reshape(N_SEQ, TOK_DEV, HEADS, HS)

    def block_step(carried, inputs):
        query_blk, key_blk, value_blk, gate_blk, ids_blk, prev_id = inputs
        query_f = query_blk.astype(jnp.float32)
        key_f = key_blk.astype(jnp.float32)
        value_f = value_blk.astype(jnp.float32)
        scores = jnp.einsum('thd,shd->hts', query_f, key_f)
        same_doc = causal & (ids_blk[:, None] == ids_blk[None, :])
        weights_intra = jnp.where(same_doc[None], scores, 0.0).astype(jnp.bfloat16)
        weights_intra = lax.optimization_barrier(weights_intra).astype(jnp.float32)
        intra_part = jnp.einsum('hts,shd->thd', weights_intra, value_f)
        carried_bf = lax.optimization_barrier(carried.astype(jnp.bfloat16)).astype(jnp.float32)
        carried_mask = (ids_blk == prev_id).astype(jnp.float32)[:, None, None]
        inter_part = jnp.einsum('thd,hde->the', query_f, carried_bf) * carried_mask
        attended = intra_part + inter_part
        scale = lax.rsqrt(lax.optimization_barrier(jnp.mean(attended * attended, axis=-1, keepdims=True)) + norm_eps)
        normed = attended * scale * gain_rows * jax.nn.sigmoid(gate_blk.astype(jnp.float32))
        head_out = normed.astype(jnp.bfloat16).reshape(TOK_DEV, HEADS * HS)
        final_id = ids_blk[-1]
        key_masked = key_f * (ids_blk == final_id).astype(jnp.float32)[:, None, None]
        summary = jnp.einsum('thd,the->hde', key_masked, value_f)
        keep_flag = (prev_id == final_id).astype(jnp.float32)
        return (summary + keep_flag * carried, head_out)
    initial = jnp.zeros((HEADS, HS, HS), jnp.float32)
    _, outputs = lax.scan(block_step, initial, (shaped(queries), shaped(key_rows), shaped(value_rows), shaped(gate_logits), doc_ids, before_ids))
    attended_all = outputs.reshape(TOKENS, HEADS * HS)
    return jnp.dot(attended_all, out_weight, preferred_element_type=jnp.float32).astype(jnp.bfloat16)
```

```python
import functools

import jax
import jax.numpy as jnp
from jax import lax
from jax.experimental import pallas as pl
from jax.experimental.pallas import tpu as pltpu
from jax.sharding import PartitionSpec as P

HS = 128
EPS = 1e-05
BOTH = ("seq", "head")
VMEM_LIMIT = 64 * 1024 * 1024
COST_SCALE = 4096
F32 = jnp.float32
BF16 = jnp.bfloat16


def params():
    return pltpu.CompilerParams(vmem_limit_bytes=VMEM_LIMIT)


def cost(flops, nbytes):
    return pl.CostEstimate(flops=flops // COST_SCALE, bytes_accessed=nbytes // COST_SCALE, transcendentals=0)


def tie(value, *before):
    return lax.optimization_barrier((value, *before))[0]


def doc_start_of(lengths_ref, position):
    def step(c, carry):
        start, found = carry
        found = jnp.where(start <= position, start, found)
        return start + lengths_ref[c], found

    _, found = lax.fori_loop(0, lengths_ref.shape[0], step, (jnp.int32(0), jnp.int32(0)))
    return found


def doc_start_rows(lengths_ref, first_pos, rows):
    positions = lax.broadcasted_iota(jnp.int32, (rows, HS), 0)
    found = jnp.full((rows, HS), -first_pos, jnp.int32)
    start = -first_pos
    for c in range(lengths_ref.shape[0]):
        found = jnp.where(start <= positions, start, found)
        start = start + lengths_ref[c]
    return found


def summary_kernel(lengths_ref, key_ref, value_ref, out_ref):
    rows = key_ref.shape[0]
    first_pos = lax.axis_index("seq") * rows
    last_start = doc_start_of(lengths_ref, first_pos + rows - 1) - first_pos
    mask = lax.broadcasted_iota(jnp.int32, (rows, HS), 0) >= last_start
    for h in range(out_ref.shape[0]):
        at = slice(h * HS, (h + 1) * HS)
        keys = jnp.where(mask, key_ref[:, at].astype(F32), 0.0).astype(BF16)
        total = lax.dot_general(keys, value_ref[:, at], (((0,), (0,)), ((), ())), preferred_element_type=F32)
        out_ref[h] = total.astype(BF16)


def pair_kernel(lengths_ref, own_ref, other_ref, out_ref, *, rows):
    index = lax.axis_index("seq")
    odd = lax.rem(index, 2)
    odd_first = (index - odd + 1) * rows
    keep = (doc_start_of(lengths_ref, odd_first + rows - 1) < odd_first).astype(F32)
    own_scale = jnp.where(odd == 1, 1.0, keep)
    other_scale = jnp.where(odd == 1, keep, 1.0)
    out_ref[...] = (own_scale * own_ref[...].astype(F32) + other_scale * other_ref[...].astype(F32)).astype(BF16)


def intra_kernel(lengths_ref, query_ref, key_ref, value_ref, out_ref, start_ref, *, tile):
    rows = query_ref.shape[0]

    @pl.when(pl.program_id(0) == 0)
    def _():
        start_ref[...] = doc_start_rows(lengths_ref, lax.axis_index("seq") * rows, rows)

    for t in range(rows // tile):
        at = pl.ds(t * tile, tile)
        query = query_ref[at, :]
        starts = start_ref[at, 0:1]
        span = (t + 1) * tile
        scores = lax.dot_general(
            query, key_ref[pl.ds(0, span), :], (((1,), (1,)), ((), ())), preferred_element_type=F32
        )
        s = lax.broadcasted_iota(jnp.int32, (tile, span), 1)
        p = lax.broadcasted_iota(jnp.int32, (tile, span), 0) + t * tile
        weights = jnp.where((s <= p) & (s >= starts), scores, 0.0).astype(BF16)
        out_ref[at, :] = jnp.dot(weights, value_ref[pl.ds(0, span), :], preferred_element_type=F32)


def finish_kernel(
    lengths_ref, query_ref, low_ref, high_ref, gate_ref, gain_ref, other_ref, *rest, rows, heads_low
):
    pair_refs, (out_ref, scalars_ref) = rest[:-2], rest[-2:]
    index = lax.axis_index("seq")
    odd = lax.rem(index, 2)
    first_pos = index * rows
    pair_first = (index - odd) * rows

    @pl.when(pl.program_id(0) == 0)
    def _():
        start, before, end = jnp.int32(0), jnp.int32(0), jnp.int32(0)
        for c in range(lengths_ref.shape[0]):
            following = start + lengths_ref[c]
            inside = start <= first_pos - 1
            before = jnp.where(inside, start, before)
            end = jnp.where(inside, following, end)
            start = following
        scalars_ref[0] = before
        scalars_ref[1] = end

    before, end = scalars_ref[0], scalars_ref[1]
    incoming = odd.astype(F32) * other_ref[0].astype(F32)
    for j, pair_ref in enumerate(pair_refs):
        live = (before < pair_first - j * 2 * rows).astype(F32)
        incoming = incoming + live * pair_ref[0].astype(F32)
    carried = incoming.astype(BF16)
    inter = jnp.dot(query_ref[...], carried, preferred_element_type=F32)
    inside = lax.broadcasted_iota(jnp.int32, (rows, HS), 0) < end - first_pos
    intra = jnp.where(pl.program_id(0) < heads_low, low_ref[...], high_ref[...])
    a = intra + jnp.where(inside, inter, 0.0)
    scale = lax.rsqrt(jnp.mean(a * a, axis=-1, keepdims=True) + EPS)
    gate = jax.nn.sigmoid(gate_ref[...].astype(F32))
    out_ref[...] = (a * scale * gain_ref[...] * gate).astype(BF16)


def merge_kernel(mine_ref, gathered_ref, out_ref):
    rows = mine_ref.shape[0]
    wide = out_ref.shape[2]
    for i in range(out_ref.shape[0]):
        out_ref[i, :rows, :] = mine_ref[:, i * wide : (i + 1) * wide]
        out_ref[i, rows:, :] = gathered_ref[:, i * wide : (i + 1) * wide]


def split_kernel(*refs):
    half = len(refs) // 3
    for i, ref in enumerate(refs[:half]):
        for j in range(2):
            refs[half + 2 * i + j][...] = ref[j : j + 1]


def partial_kernel(table_ref, own_ref, other_ref, *rest, slots, at):
    weights, (sent_ref, kept_ref, buffer_ref, sems) = rest[:slots], rest[slots:]
    width = own_ref.shape[1]
    pieces, _, columns = weights[0].shape

    def copies(slot):
        return [
            pltpu.make_async_copy(
                weights[slot].at[piece],
                buffer_ref.at[slot, :, pl.ds(piece * columns, columns)],
                sems.at[slot, piece],
            )
            for piece in range(pieces)
        ]

    @pl.when(pl.program_id(0) == 0)
    def _():
        for slot in range(slots):

            @pl.when(table_ref[at + slot] != 0)
            def _():
                for copy in copies(slot):
                    copy.start()

    for slot in range(slots):
        role = table_ref[at + slot]

        @pl.when((role != 0) & (pl.program_id(0) == 0))
        def _():
            for copy in copies(slot):
                copy.wait()

        @pl.when(role != 0)
        def _():
            total = jnp.dot(own_ref[...], buffer_ref[slot, :width, :], preferred_element_type=F32)
            total += jnp.dot(other_ref[...], buffer_ref[slot, width:, :], preferred_element_type=F32)

            @pl.when(role == 1)
            def _():
                kept_ref[...] = total

            @pl.when(role == 2)
            def _():
                sent_ref[...] = total.astype(BF16)


def add_kernel(table_ref, kept_ref, *rest, at, shares):
    received, out_ref = rest[:shares], rest[-1]

    @pl.when(table_ref[at] == 1)
    def _():
        total = kept_ref[...]
        for ref in received:
            total = total + ref[...].astype(F32)
        out_ref[...] = total.astype(BF16).reshape(out_ref.shape)

    @pl.when(table_ref[at] != 1)
    def _():
        out_ref[...] = rest[shares][...] if len(rest) > shares + 1 else jnp.zeros_like(out_ref)


def plan(n, heads, pieces):
    ring = list(range(0, n, 2)) + list(range(n - 1, 0, -2))
    spot = {s: p for p, s in enumerate(ring)}
    per_head = n // heads
    half = n // 2
    everything = tuple(range(pieces))
    wanted = [((0,), everything)]
    for k in range(1, half):
        if k < half - 1:
            wanted.append(((-k, k), everything))
        else:
            wanted += [((-k, k), (i,)) for i in everything]
    wanted += [((half,), (i,)) for i in everything]

    def block(s, slot):
        return ring[(spot[s] + slot) % n]

    def role(s, h, slot):
        owner = block(s, slot) // per_head
        if owner % 2 != h % 2:
            return 0
        return 1 if owner == h else 2

    groups = []
    for slots, chosen in wanted:
        clash = any(
            [role(s, h, slot) for slot in slots].count(r) > 1 for s in range(n) for h in range(heads) for r in (1, 2)
        )
        groups += [((slot,), chosen) for slot in slots] if clash else [(slots, chosen)]
    places, rows = [], [[] for _ in range(n * heads)]
    for slots, chosen in groups:
        places.append(len(rows[0]))
        for s in range(n):
            for h in range(heads):
                roles = [role(s, h, slot) for slot in slots]
                mine = [slot for slot, r in zip(slots, roles) if r == 1]
                column = block(s, mine[0]) % per_head if mine else 0
                if len(chosen) < pieces:
                    column = column * pieces + chosen[0]
                rows[s * heads + h] += [int(bool(mine)), column] + roles
    return ring, groups, places, rows, block


def solution(mesh):
    n, heads = mesh.shape["seq"], mesh.shape["head"]
    pairs = heads // 2
    per_head = n // heads
    half = n // 2

    def shards(queries, key_rows, value_rows, gate_logits, norm_gain, out_weight, doc_lengths):
        rows, width = queries.shape
        heads_here = width // HS
        columns = out_weight.shape[1]
        pieces = 2 if columns % 256 == 0 else 1
        part = columns // pieces
        ring, groups, places, table_rows, block = plan(n, heads, pieces)
        device = lax.axis_index("seq") * heads + lax.axis_index("head")
        table = lax.dynamic_index_in_dim(jnp.asarray(table_rows, jnp.int32), device, 0, keepdims=False)
        smem = pl.BlockSpec(memory_space=pltpu.SMEM)
        anywhere = pl.BlockSpec(memory_space=pl.ANY)
        head_block = pl.BlockSpec((rows, HS), lambda h: (0, h))
        two_heads = pl.BlockSpec((rows, 2 * HS), lambda h: (0, h))
        state_block = pl.BlockSpec((1, HS, HS), lambda h: (h, 0, 0))

        def core_of(s, slot):
            return (block(s, slot) // per_head) % 2

        def call(kernel, name, **options):
            return pl.pallas_call(kernel, compiler_params=params(), name=name, **options)

        summary = call(
            summary_kernel,
            "summary",
            grid=(heads_here // 2,),
            in_specs=[smem, two_heads, two_heads],
            out_specs=pl.BlockSpec((2, HS, HS), lambda h: (h, 0, 0)),
            out_shape=jax.ShapeDtypeStruct((heads_here, HS, HS), BF16),
            cost_estimate=cost(2 * rows * width * HS, 4 * rows * width),
        )(doc_lengths, key_rows, value_rows)

        def along(slot, step):
            target = {s: block(s, -step) for s in range(n)}
            return [
                (s * heads + 2 * y + core_of(s, slot), target[s] * heads + 2 * y + core_of(s, slot))
                for s in range(n)
                for y in range(pairs)
            ]

        gather = [
            (s * heads + 2 * y + 1 - core_of(s, 0), s * heads + 2 * y + core_of(s, 0))
            for s in range(n)
            for y in range(pairs)
        ]
        arrived = {}

        def send_on(k, i, *before):
            steps = (-1, 1) if k < half else (-1 if i % 2 == 0 else 1,)
            for step in steps:
                source = step * (k - 1)
                here = arrived.get((source, None), arrived.get((source, i)))
                if i is None or here.shape[0] == 1:
                    here = tie(here, *before)
                if i is not None and here.shape[0] > 1:
                    if (source, i) not in arrived:
                        both = [tie(arrived[x, None], *before) for x in (-source, source)]
                        split = call(
                            split_kernel,
                            "split",
                            out_shape=[jax.ShapeDtypeStruct((1, *here.shape[1:]), BF16)] * (2 * len(both)),
                            cost_estimate=cost(width * columns, 16 * width * columns),
                        )(*both)
                        for x, halves in zip((-source, source), (split[:2], split[2:])):
                            for j in range(2):
                                arrived[x, j] = halves[j]
                    here = arrived[source, i]
                arrived[half if k == half else step * k, i] = lax.ppermute(here, BOTH, along(source, step))

        def there(k, i):
            return [arrived[key] for key in ((-k, i), (k, i)) if key in arrived]

        gathered = lax.ppermute(out_weight, BOTH, gather)
        merged = call(
            merge_kernel,
            "merge",
            out_shape=jax.ShapeDtypeStruct((pieces, 2 * width, part), BF16),
            cost_estimate=cost(width * part, 8 * width * columns),
        )(out_weight, tie(gathered, summary))
        arrived[0, None] = merged

        other_state = lax.ppermute(summary, "seq", [(s, s ^ 1) for s in range(n)])

        def intra_of(first, count, *before):
            block_at = pl.BlockSpec((rows, HS), lambda h: (0, first + h))
            return call(
                functools.partial(intra_kernel, tile=256),
                "intra",
                grid=(count,),
                in_specs=[smem, block_at, block_at, block_at],
                out_specs=head_block,
                out_shape=jax.ShapeDtypeStruct((rows, count * HS), F32),
                scratch_shapes=[pltpu.VMEM((rows, HS), jnp.int32)],
                cost_estimate=cost(4 * rows * rows * count * HS, 10 * rows * count * HS),
            )(tie(doc_lengths, *before), queries, key_rows, value_rows)

        count = heads_here // 2
        whole_state = pl.BlockSpec((heads_here, HS, HS), lambda: (0, 0, 0))
        pair_state = call(
            functools.partial(pair_kernel, rows=rows),
            "pair_state",
            in_specs=[smem, whole_state, whole_state],
            out_specs=whole_state,
            out_shape=jax.ShapeDtypeStruct((heads_here, HS, HS), BF16),
            cost_estimate=cost(heads_here * HS * HS, 6 * heads_here * HS * HS),
        )(doc_lengths, tie(summary, merged), other_state)
        earlier = [
            lax.ppermute(pair_state, "seq", [(s, s + 2 * d) for s in range(n - 2 * d)]) for d in range(1, n // 4 + 1)
        ]
        intra_low = intra_of(0, count, pair_state)
        intra_high = intra_of(count, count, intra_low)
        send_on(1, None, *earlier)
        for k in range(2, min(3, half - 1)):
            send_on(k, None, intra_high)

        low = pl.BlockSpec((rows, HS), lambda h: (0, jnp.minimum(h, count - 1)))
        high = pl.BlockSpec((rows, HS), lambda h: (0, jnp.maximum(h - count, 0)))
        head_out = call(
            functools.partial(finish_kernel, rows=rows, heads_low=count),
            "finish",
            grid=(heads_here,),
            in_specs=[smem, head_block, low, high, head_block, pl.BlockSpec((1, HS), lambda h: (0, h)), state_block]
            + [state_block] * len(earlier),
            out_specs=head_block,
            out_shape=jax.ShapeDtypeStruct((rows, width), BF16),
            scratch_shapes=[pltpu.SMEM((2,), jnp.int32)],
            cost_estimate=cost(2 * rows * width * HS, 12 * rows * width),
        )(
            doc_lengths,
            queries,
            intra_low,
            intra_high,
            gate_logits,
            norm_gain.reshape(1, width),
            other_state,
            *earlier,
        )
        head_other = lax.ppermute(head_out, "head", [(h, h ^ 1) for h in range(heads)])

        tile = min(rows, 512)
        by_columns = part % 128 == 0
        out = []
        out_dims = (rows, per_head * columns) if by_columns else (per_head, rows, columns)
        row_tile = pl.BlockSpec((tile, width), lambda i: (i, 0))

        def share(g, *before):
            (slots, chosen), at = groups[g], places[g]
            wide = part * len(chosen)
            weights = [arrived[slot, None if (slot, None) in arrived else chosen[0]] for slot in slots]
            sent, kept = call(
                functools.partial(partial_kernel, slots=len(slots), at=at + 2),
                "partial",
                grid=(rows // tile,),
                in_specs=[smem, row_tile, row_tile] + [anywhere] * len(weights),
                out_specs=[pl.BlockSpec((tile, wide), lambda i: (i, 0))] * 2,
                out_shape=[jax.ShapeDtypeStruct((rows, wide), BF16), jax.ShapeDtypeStruct((rows, wide), F32)],
                scratch_shapes=[
                    pltpu.VMEM((len(slots), 2 * width, wide), BF16),
                    pltpu.SemaphoreType.DMA((len(slots), len(chosen))),
                ],
                cost_estimate=cost(4 * rows * width * wide, 4 * rows * width + 10 * rows * wide),
            )(tie(table, *before), head_out, head_other, *weights)
            received = []
            for d in range(1, pairs):
                to_owner = []
                for s in range(n):
                    for slot in slots:
                        y, core = divmod(block(s, slot) // per_head, 2)
                        to_owner.append((s * heads + 2 * ((y + d) % pairs) + core, s * heads + 2 * y + core))
                received.append(lax.ppermute(sent, BOTH, to_owner))
            return kept, received, sent

        def add(g, shares, *before):
            nonlocal out
            (slots, chosen), at = groups[g], places[g]
            kept, received, _ = shares
            wide = part * len(chosen)
            tiles = pl.BlockSpec((tile, wide), lambda i, t: (i * t[at], 0))
            if by_columns:
                target = pl.BlockSpec((tile, wide), lambda i, t: (i * t[at], t[at + 1]))
            else:
                target = pl.BlockSpec((1, tile, wide), lambda i, t: (t[at + 1], i * t[at], 0))
            out = [
                call(
                    functools.partial(add_kernel, at=at, shares=len(received)),
                    "add_shares",
                    grid_spec=pltpu.PrefetchScalarGridSpec(
                        num_scalar_prefetch=1,
                        grid=(rows // tile,),
                        in_specs=[tiles] * (1 + len(received)) + [target] * len(out),
                        out_specs=target,
                    ),
                    out_shape=jax.ShapeDtypeStruct(out_dims, BF16),
                    input_output_aliases={2 + len(received): 0} if out else {},
                    cost_estimate=cost(2 * rows * wide, 10 * rows * wide),
                )(tie(table, *before), kept, *received, *out)
            ]

        waiting, last = [], [head_out]
        for g, (slots, chosen) in enumerate(groups):
            k, i = abs(slots[0]), chosen[0]
            arrival = []
            if k == 2 and slots[0] < 0:
                if half > 4:
                    send_on(3, None, *last)
                else:
                    for j in range(pieces):
                        send_on(3, j, *last)
            elif 2 < k < half - 1 and slots[0] < 0:
                arrival = there(k, None)
                if k + 1 < half - 1:
                    send_on(k + 1, None, *last)
                else:
                    for j in range(pieces):
                        send_on(k + 1, j, *last)
            elif k == half - 1 and (half, i) not in arrived:
                send_on(half, i, *last)
            shares = share(g, *last, *arrival)
            waiting.append((g, shares))
            last = [shares[2]]
            if len(waiting) > 2:
                add(*waiting.pop(0), *last)
                last = out
        for g, pending in waiting:
            add(g, pending)
        out = out[0]
        if not by_columns:
            out = jnp.transpose(out, (1, 0, 2)).reshape(rows, per_head * columns)
        return out

    return jax.shard_map(
        shards,
        mesh=mesh,
        in_specs=(
            P("seq", "head"),
            P("seq", "head"),
            P("seq", "head"),
            P("seq", "head"),
            P("head"),
            P("head", "seq"),
            P(),
        ),
        out_specs=P("seq", "head"),
        check_vma=False,
    )
```

```python
import functools

import jax
import jax.numpy as jnp
from jax import lax
from jax.experimental import pallas as pl
from jax.experimental.pallas import tpu as pltpu
from jax.sharding import PartitionSpec as P

HS = 128
EPS = 1e-05
BOTH = ("seq", "head")
VMEM_LIMIT = 64 * 1024 * 1024
COST_SCALE = 4096
F32 = jnp.float32
BF16 = jnp.bfloat16


def params():
    return pltpu.CompilerParams(vmem_limit_bytes=VMEM_LIMIT)


def cost(flops, nbytes):
    return pl.CostEstimate(flops=flops // COST_SCALE, bytes_accessed=nbytes // COST_SCALE, transcendentals=0)


def tie(value, *before):
    return lax.optimization_barrier((value, *before))[0]


def doc_start_of(lengths_ref, position):
    def step(c, carry):
        start, found = carry
        found = jnp.where(start <= position, start, found)
        return start + lengths_ref[c], found

    _, found = lax.fori_loop(0, lengths_ref.shape[0], step, (jnp.int32(0), jnp.int32(0)))
    return found


def doc_start_rows(lengths_ref, first_pos, rows):
    positions = lax.broadcasted_iota(jnp.int32, (rows, HS), 0)
    found = jnp.full((rows, HS), -first_pos, jnp.int32)
    start = -first_pos
    for c in range(lengths_ref.shape[0]):
        found = jnp.where(start <= positions, start, found)
        start = start + lengths_ref[c]
    return found


def summary_kernel(lengths_ref, key_ref, value_ref, out_ref):
    rows = key_ref.shape[0]
    first_pos = lax.axis_index("seq") * rows
    last_start = doc_start_of(lengths_ref, first_pos + rows - 1) - first_pos
    mask = lax.broadcasted_iota(jnp.int32, (rows, HS), 0) >= last_start
    for h in range(out_ref.shape[0]):
        at = slice(h * HS, (h + 1) * HS)
        keys = jnp.where(mask, key_ref[:, at].astype(F32), 0.0).astype(BF16)
        total = lax.dot_general(keys, value_ref[:, at], (((0,), (0,)), ((), ())), preferred_element_type=F32)
        out_ref[h] = total.astype(BF16)


def pair_kernel(lengths_ref, own_ref, other_ref, out_ref, *, rows):
    index = lax.axis_index("seq")
    odd = lax.rem(index, 2)
    odd_first = (index - odd + 1) * rows
    keep = (doc_start_of(lengths_ref, odd_first + rows - 1) < odd_first).astype(F32)
    own_scale = jnp.where(odd == 1, 1.0, keep)
    other_scale = jnp.where(odd == 1, keep, 1.0)
    out_ref[...] = (own_scale * own_ref[...].astype(F32) + other_scale * other_ref[...].astype(F32)).astype(BF16)


def intra_kernel(lengths_ref, query_ref, key_ref, value_ref, out_ref, start_ref, *, tile):
    rows = query_ref.shape[0]

    @pl.when(pl.program_id(0) == 0)
    def _():
        start_ref[...] = doc_start_rows(lengths_ref, lax.axis_index("seq") * rows, rows)

    for t in range(rows // tile):
        at = pl.ds(t * tile, tile)
        query = query_ref[at, :]
        starts = start_ref[at, 0:1]
        span = (t + 1) * tile
        scores = lax.dot_general(
            query, key_ref[pl.ds(0, span), :], (((1,), (1,)), ((), ())), preferred_element_type=F32
        )
        s = lax.broadcasted_iota(jnp.int32, (tile, span), 1)
        p = lax.broadcasted_iota(jnp.int32, (tile, span), 0) + t * tile
        weights = jnp.where((s <= p) & (s >= starts), scores, 0.0).astype(BF16)
        out_ref[at, :] = jnp.dot(weights, value_ref[pl.ds(0, span), :], preferred_element_type=F32)


def finish_kernel(
    lengths_ref, query_ref, low_ref, high_ref, gate_ref, gain_ref, other_ref, *rest, rows, heads_low
):
    pair_refs, (out_ref, scalars_ref) = rest[:-2], rest[-2:]
    index = lax.axis_index("seq")
    odd = lax.rem(index, 2)
    first_pos = index * rows
    pair_first = (index - odd) * rows

    @pl.when(pl.program_id(0) == 0)
    def _():
        start, before, end = jnp.int32(0), jnp.int32(0), jnp.int32(0)
        for c in range(lengths_ref.shape[0]):
            following = start + lengths_ref[c]
            inside = start <= first_pos - 1
            before = jnp.where(inside, start, before)
            end = jnp.where(inside, following, end)
            start = following
        scalars_ref[0] = before
        scalars_ref[1] = end

    before, end = scalars_ref[0], scalars_ref[1]
    incoming = odd.astype(F32) * other_ref[0].astype(F32)
    for j, pair_ref in enumerate(pair_refs):
        live = (before < pair_first - j * 2 * rows).astype(F32)
        incoming = incoming + live * pair_ref[0].astype(F32)
    carried = incoming.astype(BF16)
    inter = jnp.dot(query_ref[...], carried, preferred_element_type=F32)
    inside = lax.broadcasted_iota(jnp.int32, (rows, HS), 0) < end - first_pos
    intra = jnp.where(pl.program_id(0) < heads_low, low_ref[...], high_ref[...])
    a = intra + jnp.where(inside, inter, 0.0)
    scale = lax.rsqrt(jnp.mean(a * a, axis=-1, keepdims=True) + EPS)
    gate = jax.nn.sigmoid(gate_ref[...].astype(F32))
    out_ref[...] = (a * scale * gain_ref[...] * gate).astype(BF16)


def merge_kernel(mine_ref, gathered_ref, out_ref):
    rows = mine_ref.shape[0]
    wide = out_ref.shape[2]
    for i in range(out_ref.shape[0]):
        out_ref[i, :rows, :] = mine_ref[:, i * wide : (i + 1) * wide]
        out_ref[i, rows:, :] = gathered_ref[:, i * wide : (i + 1) * wide]


def split_kernel(*refs):
    half = len(refs) // 3
    for i, ref in enumerate(refs[:half]):
        for j in range(2):
            refs[half + 2 * i + j][...] = ref[j : j + 1]


def partial_kernel(table_ref, own_ref, other_ref, *rest, slots, at):
    weights, (sent_ref, kept_ref, buffer_ref, sems) = rest[:slots], rest[slots:]
    pieces, _, columns = weights[0].shape

    def copies(slot):
        return [
            pltpu.make_async_copy(
                weights[slot].at[piece],
                buffer_ref.at[slot, :, pl.ds(piece * columns, columns)],
                sems.at[slot, piece],
            )
            for piece in range(pieces)
        ]

    @pl.when(pl.program_id(0) == 0)
    def _():
        for slot in range(slots):

            @pl.when(table_ref[at + slot] != 0)
            def _():
                for copy in copies(slot):
                    copy.start()

    for slot in range(slots):
        role = table_ref[at + slot]

        @pl.when((role != 0) & (pl.program_id(0) == 0))
        def _():
            for copy in copies(slot):
                copy.wait()

        @pl.when(role != 0)
        def _():
            features = jnp.concatenate([own_ref[...], other_ref[...]], axis=1)
            total = jnp.dot(features, buffer_ref[slot], preferred_element_type=F32)

            @pl.when(role == 1)
            def _():
                kept_ref[...] = total

            @pl.when(role == 2)
            def _():
                sent_ref[...] = total.astype(BF16)


def add_kernel(table_ref, kept_ref, *rest, at, shares, tile):
    received, (out_ref, kept_buffer, buffers, sum_buffer, sems) = rest[:shares], rest[-5:]
    rows, wide = kept_ref.shape
    tiles = rows // tile
    column = table_ref[at + 1]

    def copies_in(t):
        here = pl.ds(t * tile, tile)
        return [pltpu.make_async_copy(kept_ref.at[here, :], kept_buffer.at[here, :], sems.at[t, 0])] + [
            pltpu.make_async_copy(ref.at[here, :], buffers.at[i, here, :], sems.at[t, 1 + i])
            for i, ref in enumerate(received)
        ]

    def copy_out(t):
        here = pl.ds(t * tile, tile)
        if len(out_ref.shape) == 2:
            place = out_ref.at[here, pl.ds(pl.multiple_of(column * wide, 128), wide)]
        else:
            place = out_ref.at[column, here, :]
        return pltpu.make_async_copy(sum_buffer.at[here, :], place, sems.at[t, 1 + shares])

    @pl.when(table_ref[at] == 1)
    def _():
        for t in range(tiles):
            for copy in copies_in(t):
                copy.start()
        for t in range(tiles):
            for copy in copies_in(t):
                copy.wait()
            here = pl.ds(t * tile, tile)
            total = kept_buffer[here, :]
            for i in range(shares):
                total = total + buffers[i, here, :].astype(F32)
            sum_buffer[here, :] = total.astype(BF16)
            copy_out(t).start()
        for t in range(tiles):
            copy_out(t).wait()


def plan(n, heads, pieces):
    ring = list(range(0, n, 2)) + list(range(n - 1, 0, -2))
    spot = {s: p for p, s in enumerate(ring)}
    per_head = n // heads
    half = n // 2
    everything = tuple(range(pieces))
    wanted = [((0,), everything)]
    for k in range(1, half):
        if k < half - 1:
            wanted.append(((-k, k), everything))
        else:
            wanted += [((-k, k), (i,)) for i in everything]
    wanted += [((half,), (i,)) for i in everything]

    def block(s, slot):
        return ring[(spot[s] + slot) % n]

    def role(s, h, slot):
        owner = block(s, slot) // per_head
        if owner % 2 != h % 2:
            return 0
        return 1 if owner == h else 2

    groups = []
    for slots, chosen in wanted:
        clash = any(
            [role(s, h, slot) for slot in slots].count(r) > 1 for s in range(n) for h in range(heads) for r in (1, 2)
        )
        groups += [((slot,), chosen) for slot in slots] if clash else [(slots, chosen)]
    places, rows = [], [[] for _ in range(n * heads)]
    for slots, chosen in groups:
        places.append(len(rows[0]))
        for s in range(n):
            for h in range(heads):
                roles = [role(s, h, slot) for slot in slots]
                mine = [slot for slot, r in zip(slots, roles) if r == 1]
                column = block(s, mine[0]) % per_head if mine else 0
                if len(chosen) < pieces:
                    column = column * pieces + chosen[0]
                rows[s * heads + h] += [int(bool(mine)), column] + roles
    return ring, groups, places, rows, block


def solution(mesh):
    n, heads = mesh.shape["seq"], mesh.shape["head"]
    pairs = heads // 2
    per_head = n // heads
    half = n // 2

    def shards(queries, key_rows, value_rows, gate_logits, norm_gain, out_weight, doc_lengths):
        rows, width = queries.shape
        heads_here = width // HS
        columns = out_weight.shape[1]
        pieces = 2 if columns % 256 == 0 else 1
        part = columns // pieces
        ring, groups, places, table_rows, block = plan(n, heads, pieces)
        device = lax.axis_index("seq") * heads + lax.axis_index("head")
        table = lax.dynamic_index_in_dim(jnp.asarray(table_rows, jnp.int32), device, 0, keepdims=False)
        smem = pl.BlockSpec(memory_space=pltpu.SMEM)
        anywhere = pl.BlockSpec(memory_space=pl.ANY)
        head_block = pl.BlockSpec((rows, HS), lambda h: (0, h))
        two_heads = pl.BlockSpec((rows, 2 * HS), lambda h: (0, h))
        state_block = pl.BlockSpec((1, HS, HS), lambda h: (h, 0, 0))

        def core_of(s, slot):
            return (block(s, slot) // per_head) % 2

        def call(kernel, name, **options):
            return pl.pallas_call(kernel, compiler_params=params(), name=name, **options)

        summary = call(
            summary_kernel,
            "summary",
            grid=(heads_here // 2,),
            in_specs=[smem, two_heads, two_heads],
            out_specs=pl.BlockSpec((2, HS, HS), lambda h: (h, 0, 0)),
            out_shape=jax.ShapeDtypeStruct((heads_here, HS, HS), BF16),
            cost_estimate=cost(2 * rows * width * HS, 4 * rows * width),
        )(doc_lengths, key_rows, value_rows)

        def along(slot, step):
            target = {s: block(s, -step) for s in range(n)}
            return [
                (s * heads + 2 * y + core_of(s, slot), target[s] * heads + 2 * y + core_of(s, slot))
                for s in range(n)
                for y in range(pairs)
            ]

        gather = [
            (s * heads + 2 * y + 1 - core_of(s, 0), s * heads + 2 * y + core_of(s, 0))
            for s in range(n)
            for y in range(pairs)
        ]
        arrived = {}

        def send_on(k, i, *before):
            steps = (-1, 1) if k < half else (-1 if i % 2 == 0 else 1,)
            for step in steps:
                source = step * (k - 1)
                here = arrived.get((source, None), arrived.get((source, i)))
                if i is None or here.shape[0] == 1:
                    here = tie(here, *before)
                if i is not None and here.shape[0] > 1:
                    if (source, i) not in arrived:
                        both = [tie(arrived[x, None], *before) for x in (-source, source)]
                        split = call(
                            split_kernel,
                            "split",
                            out_shape=[jax.ShapeDtypeStruct((1, *here.shape[1:]), BF16)] * (2 * len(both)),
                            cost_estimate=cost(width * columns, 16 * width * columns),
                        )(*both)
                        for x, halves in zip((-source, source), (split[:2], split[2:])):
                            for j in range(2):
                                arrived[x, j] = halves[j]
                    here = arrived[source, i]
                arrived[half if k == half else step * k, i] = lax.ppermute(here, BOTH, along(source, step))

        def there(k, i):
            return [arrived[key] for key in ((-k, i), (k, i)) if key in arrived]

        gathered = lax.ppermute(out_weight, BOTH, gather)
        merged = call(
            merge_kernel,
            "merge",
            out_shape=jax.ShapeDtypeStruct((pieces, 2 * width, part), BF16),
            cost_estimate=cost(width * part, 8 * width * columns),
        )(out_weight, tie(gathered, summary))
        arrived[0, None] = merged

        other_state = lax.ppermute(summary, "seq", [(s, s ^ 1) for s in range(n)])
        send_on(1, None, other_state)

        def intra_of(first, count, *before):
            block_at = pl.BlockSpec((rows, HS), lambda h: (0, first + h))
            return call(
                functools.partial(intra_kernel, tile=256),
                "intra",
                grid=(count,),
                in_specs=[smem, block_at, block_at, block_at],
                out_specs=head_block,
                out_shape=jax.ShapeDtypeStruct((rows, count * HS), F32),
                scratch_shapes=[pltpu.VMEM((rows, HS), jnp.int32)],
                cost_estimate=cost(4 * rows * rows * count * HS, 10 * rows * count * HS),
            )(tie(doc_lengths, *before), queries, key_rows, value_rows)

        count = heads_here // 2
        whole_state = pl.BlockSpec((heads_here, HS, HS), lambda: (0, 0, 0))
        pair_state = call(
            functools.partial(pair_kernel, rows=rows),
            "pair_state",
            in_specs=[smem, whole_state, whole_state],
            out_specs=whole_state,
            out_shape=jax.ShapeDtypeStruct((heads_here, HS, HS), BF16),
            cost_estimate=cost(heads_here * HS * HS, 6 * heads_here * HS * HS),
        )(doc_lengths, tie(summary, merged), other_state)
        earlier = [
            lax.ppermute(pair_state, "seq", [(s, s + 2 * d) for s in range(n - 2 * d)]) for d in range(1, n // 4 + 1)
        ]
        intra_low = intra_of(0, count, pair_state)
        intra_high = intra_of(count, count, intra_low)
        for k in range(2, min(3, half - 1)):
            send_on(k, None, intra_high, *earlier)

        low = pl.BlockSpec((rows, HS), lambda h: (0, jnp.minimum(h, count - 1)))
        high = pl.BlockSpec((rows, HS), lambda h: (0, jnp.maximum(h - count, 0)))
        head_out = call(
            functools.partial(finish_kernel, rows=rows, heads_low=count),
            "finish",
            grid=(heads_here,),
            in_specs=[smem, head_block, low, high, head_block, pl.BlockSpec((1, HS), lambda h: (0, h)), state_block]
            + [state_block] * len(earlier),
            out_specs=head_block,
            out_shape=jax.ShapeDtypeStruct((rows, width), BF16),
            scratch_shapes=[pltpu.SMEM((2,), jnp.int32)],
            cost_estimate=cost(2 * rows * width * HS, 12 * rows * width),
        )(
            doc_lengths,
            queries,
            intra_low,
            intra_high,
            gate_logits,
            norm_gain.reshape(1, width),
            other_state,
            *earlier,
        )
        head_other = lax.ppermute(head_out, "head", [(h, h ^ 1) for h in range(heads)])

        tile = min(rows, 512)
        by_columns = part % 128 == 0
        out = []
        out_dims = (rows, per_head * columns) if by_columns else (per_head, rows, columns)
        row_tile = pl.BlockSpec((tile, width), lambda i: (i, 0))

        def share(g, *before):
            (slots, chosen), at = groups[g], places[g]
            wide = part * len(chosen)
            weights = [arrived[slot, None if (slot, None) in arrived else chosen[0]] for slot in slots]
            sent, kept = call(
                functools.partial(partial_kernel, slots=len(slots), at=at + 2),
                "partial",
                grid=(rows // tile,),
                in_specs=[smem, row_tile, row_tile] + [anywhere] * len(weights),
                out_specs=[pl.BlockSpec((tile, wide), lambda i: (i, 0))] * 2,
                out_shape=[jax.ShapeDtypeStruct((rows, wide), BF16), jax.ShapeDtypeStruct((rows, wide), F32)],
                scratch_shapes=[
                    pltpu.VMEM((len(slots), 2 * width, wide), BF16),
                    pltpu.SemaphoreType.DMA((len(slots), len(chosen))),
                ],
                cost_estimate=cost(4 * rows * width * wide, 4 * rows * width + 10 * rows * wide),
            )(tie(table, *before), head_out, head_other, *weights)
            received = []
            for d in range(1, pairs):
                to_owner = []
                for s in range(n):
                    for slot in slots:
                        y, core = divmod(block(s, slot) // per_head, 2)
                        to_owner.append((s * heads + 2 * ((y + d) % pairs) + core, s * heads + 2 * y + core))
                received.append(lax.ppermute(sent, BOTH, to_owner))
            return kept, received, sent

        def add(g, shares, *before):
            nonlocal out
            (slots, chosen), at = groups[g], places[g]
            kept, received, _ = shares
            wide = part * len(chosen)
            few = min(rows, 256)
            out = [
                call(
                    functools.partial(add_kernel, at=at, shares=len(received), tile=few),
                    "add_shares",
                    in_specs=[smem] + [anywhere] * (1 + len(received) + len(out)),
                    out_specs=anywhere,
                    out_shape=jax.ShapeDtypeStruct(out_dims, BF16),
                    input_output_aliases={2 + len(received): 0} if out else {},
                    scratch_shapes=[
                        pltpu.VMEM((rows, wide), F32),
                        pltpu.VMEM((len(received), rows, wide), BF16),
                        pltpu.VMEM((rows, wide), BF16),
                        pltpu.SemaphoreType.DMA((rows // few, 2 + len(received))),
                    ],
                    cost_estimate=cost(2 * rows * wide, 10 * rows * wide),
                )(tie(table, *before), kept, *received, *out)
            ]

        waiting, last = [], [head_out]
        near = [g for g, (slots, _) in enumerate(groups) if abs(slots[0]) == 1]
        order = near + [g for g in range(len(groups)) if g not in near]
        for g in order:
            slots, chosen = groups[g]
            k, i = abs(slots[0]), chosen[0]
            arrival = []
            if k == 2 and slots[0] < 0:
                if half > 4:
                    send_on(3, None, *last)
                else:
                    for j in range(pieces):
                        send_on(3, j, *last)
            elif 2 < k < half - 1 and slots[0] < 0:
                arrival = there(k, None)
                if k + 1 < half - 1:
                    send_on(k + 1, None, *last)
                else:
                    for j in range(pieces):
                        send_on(k + 1, j, *last)
            elif k == half - 1 and (half, i) not in arrived:
                send_on(half, i, *last)
            shares = share(g, *last, *arrival)
            waiting.append((g, shares))
            last = [shares[2]]
            if len(waiting) > 2:
                add(*waiting.pop(0), *last)
                last = out
        for g, pending in waiting:
            add(g, pending)
        out = out[0]
        if not by_columns:
            out = jnp.transpose(out, (1, 0, 2)).reshape(rows, per_head * columns)
        return out

    return jax.shard_map(
        shards,
        mesh=mesh,
        in_specs=(
            P("seq", "head"),
            P("seq", "head"),
            P("seq", "head"),
            P("seq", "head"),
            P("head"),
            P("head", "seq"),
            P(),
        ),
        out_specs=P("seq", "head"),
        check_vma=False,
    )
```

```python
import functools

import jax
import jax.numpy as jnp
from jax import lax
from jax.experimental import pallas as pl
from jax.experimental.pallas import tpu as pltpu
from jax.sharding import PartitionSpec as P

HS = 128
EPS = 1e-05
BOTH = ("seq", "head")
VMEM_LIMIT = 64 * 1024 * 1024
COST_SCALE = 4096
F32 = jnp.float32
BF16 = jnp.bfloat16


def params():
    return pltpu.CompilerParams(vmem_limit_bytes=VMEM_LIMIT)


def cost(flops, nbytes):
    return pl.CostEstimate(flops=flops // COST_SCALE, bytes_accessed=nbytes // COST_SCALE, transcendentals=0)


def tie(value, *before):
    return lax.optimization_barrier((value, *before))[0]


def doc_start_of(lengths_ref, position):
    def step(c, carry):
        start, found = carry
        found = jnp.where(start <= position, start, found)
        return start + lengths_ref[c], found

    _, found = lax.fori_loop(0, lengths_ref.shape[0], step, (jnp.int32(0), jnp.int32(0)))
    return found


def doc_start_rows(lengths_ref, first_pos, rows):
    positions = lax.broadcasted_iota(jnp.int32, (rows, HS), 0)
    found = jnp.full((rows, HS), -first_pos, jnp.int32)
    start = -first_pos
    for c in range(lengths_ref.shape[0]):
        found = jnp.where(start <= positions, start, found)
        start = start + lengths_ref[c]
    return found


def summary_kernel(lengths_ref, key_ref, value_ref, out_ref):
    rows = key_ref.shape[0]
    first_pos = lax.axis_index("seq") * rows
    last_start = doc_start_of(lengths_ref, first_pos + rows - 1) - first_pos
    mask = lax.broadcasted_iota(jnp.int32, (rows, HS), 0) >= last_start
    for h in range(out_ref.shape[0]):
        at = slice(h * HS, (h + 1) * HS)
        keys = jnp.where(mask, key_ref[:, at].astype(F32), 0.0).astype(BF16)
        total = lax.dot_general(keys, value_ref[:, at], (((0,), (0,)), ((), ())), preferred_element_type=F32)
        out_ref[h] = total.astype(BF16)


def pair_kernel(lengths_ref, own_ref, other_ref, out_ref, *, rows):
    index = lax.axis_index("seq")
    odd = lax.rem(index, 2)
    odd_first = (index - odd + 1) * rows
    keep = (doc_start_of(lengths_ref, odd_first + rows - 1) < odd_first).astype(F32)
    own_scale = jnp.where(odd == 1, 1.0, keep)
    other_scale = jnp.where(odd == 1, keep, 1.0)
    out_ref[...] = (own_scale * own_ref[...].astype(F32) + other_scale * other_ref[...].astype(F32)).astype(BF16)


def intra_kernel(lengths_ref, query_ref, key_ref, value_ref, out_ref, start_ref, *, tile):
    rows = query_ref.shape[0]

    @pl.when(pl.program_id(0) == 0)
    def _():
        start_ref[...] = doc_start_rows(lengths_ref, lax.axis_index("seq") * rows, rows)

    for t in range(rows // tile):
        at = pl.ds(t * tile, tile)
        query = query_ref[at, :]
        starts = start_ref[at, 0:1]
        span = (t + 1) * tile
        scores = lax.dot_general(
            query, key_ref[pl.ds(0, span), :], (((1,), (1,)), ((), ())), preferred_element_type=F32
        )
        s = lax.broadcasted_iota(jnp.int32, (tile, span), 1)
        p = lax.broadcasted_iota(jnp.int32, (tile, span), 0) + t * tile
        weights = jnp.where((s <= p) & (s >= starts), scores, 0.0).astype(BF16)
        out_ref[at, :] = jnp.dot(weights, value_ref[pl.ds(0, span), :], preferred_element_type=F32)


def finish_kernel(
    lengths_ref, query_ref, low_ref, high_ref, gate_ref, gain_ref, other_ref, *rest, rows, heads_low
):
    pair_refs, (out_ref, scalars_ref) = rest[:-2], rest[-2:]
    index = lax.axis_index("seq")
    odd = lax.rem(index, 2)
    first_pos = index * rows
    pair_first = (index - odd) * rows

    @pl.when(pl.program_id(0) == 0)
    def _():
        start, before, end = jnp.int32(0), jnp.int32(0), jnp.int32(0)
        for c in range(lengths_ref.shape[0]):
            following = start + lengths_ref[c]
            inside = start <= first_pos - 1
            before = jnp.where(inside, start, before)
            end = jnp.where(inside, following, end)
            start = following
        scalars_ref[0] = before
        scalars_ref[1] = end

    before, end = scalars_ref[0], scalars_ref[1]
    inside = lax.broadcasted_iota(jnp.int32, (rows, HS), 0) < end - first_pos
    is_low = pl.program_id(0) < heads_low
    for h in range(other_ref.shape[0]):
        at = slice(h * HS, (h + 1) * HS)
        incoming = odd.astype(F32) * other_ref[h].astype(F32)
        for j, pair_ref in enumerate(pair_refs):
            live = (before < pair_first - j * 2 * rows).astype(F32)
            incoming = incoming + live * pair_ref[h].astype(F32)
        inter = jnp.dot(query_ref[:, at], incoming.astype(BF16), preferred_element_type=F32)
        intra = jnp.where(is_low, low_ref[:, at], high_ref[:, at])
        a = intra + jnp.where(inside, inter, 0.0)
        scale = lax.rsqrt(jnp.mean(a * a, axis=-1, keepdims=True) + EPS)
        gate = jax.nn.sigmoid(gate_ref[:, at].astype(F32))
        out_ref[:, at] = (a * scale * gain_ref[:, at] * gate).astype(BF16)


def merge_kernel(mine_ref, gathered_ref, out_ref):
    rows = mine_ref.shape[0]
    wide = out_ref.shape[2]
    for i in range(out_ref.shape[0]):
        out_ref[i, :rows, :] = mine_ref[:, i * wide : (i + 1) * wide]
        out_ref[i, rows:, :] = gathered_ref[:, i * wide : (i + 1) * wide]


def split_kernel(*refs):
    half = len(refs) // 3
    for i, ref in enumerate(refs[:half]):
        for j in range(2):
            refs[half + 2 * i + j][...] = ref[j : j + 1]


def partial_kernel(table_ref, own_ref, other_ref, *rest, slots, at):
    weights, (sent_ref, kept_ref, buffer_ref, sems) = rest[:slots], rest[slots:]
    pieces, _, columns = weights[0].shape

    def copies(slot):
        return [
            pltpu.make_async_copy(
                weights[slot].at[piece],
                buffer_ref.at[slot, :, pl.ds(piece * columns, columns)],
                sems.at[slot, piece],
            )
            for piece in range(pieces)
        ]

    @pl.when(pl.program_id(0) == 0)
    def _():
        for slot in range(slots):

            @pl.when(table_ref[at + slot] != 0)
            def _():
                for copy in copies(slot):
                    copy.start()

    for slot in range(slots):
        role = table_ref[at + slot]

        @pl.when((role != 0) & (pl.program_id(0) == 0))
        def _():
            for copy in copies(slot):
                copy.wait()

        @pl.when(role != 0)
        def _():
            features = jnp.concatenate([own_ref[...], other_ref[...]], axis=1)
            total = jnp.dot(features, buffer_ref[slot], preferred_element_type=F32)

            @pl.when(role == 1)
            def _():
                kept_ref[...] = total

            @pl.when(role == 2)
            def _():
                sent_ref[...] = total.astype(BF16)


def add_kernel(table_ref, kept_ref, *rest, at, shares, tile):
    received, (out_ref, kept_buffer, buffers, sum_buffer, sems) = rest[:shares], rest[-5:]
    rows, wide = kept_ref.shape
    tiles = rows // tile
    column = table_ref[at + 1]

    def copies_in(t):
        here = pl.ds(t * tile, tile)
        return [pltpu.make_async_copy(kept_ref.at[here, :], kept_buffer.at[here, :], sems.at[t, 0])] + [
            pltpu.make_async_copy(ref.at[here, :], buffers.at[i, here, :], sems.at[t, 1 + i])
            for i, ref in enumerate(received)
        ]

    def copy_out(t):
        here = pl.ds(t * tile, tile)
        if len(out_ref.shape) == 2:
            place = out_ref.at[here, pl.ds(pl.multiple_of(column * wide, 128), wide)]
        else:
            place = out_ref.at[column, here, :]
        return pltpu.make_async_copy(sum_buffer.at[here, :], place, sems.at[t, 1 + shares])

    @pl.when(table_ref[at] == 1)
    def _():
        for t in range(tiles):
            for copy in copies_in(t):
                copy.start()
        for t in range(tiles):
            for copy in copies_in(t):
                copy.wait()
            here = pl.ds(t * tile, tile)
            total = kept_buffer[here, :]
            for i in range(shares):
                total = total + buffers[i, here, :].astype(F32)
            sum_buffer[here, :] = total.astype(BF16)
            copy_out(t).start()
        for t in range(tiles):
            copy_out(t).wait()


def plan(n, heads, pieces):
    ring = list(range(0, n, 2)) + list(range(n - 1, 0, -2))
    spot = {s: p for p, s in enumerate(ring)}
    per_head = n // heads
    half = n // 2
    everything = tuple(range(pieces))
    wanted = [((0,), everything)]
    for k in range(1, half):
        if k < half - 1:
            wanted.append(((-k, k), everything))
        else:
            wanted += [((-k, k), (i,)) for i in everything]
    wanted += [((half,), (i,)) for i in everything]

    def block(s, slot):
        return ring[(spot[s] + slot) % n]

    def role(s, h, slot):
        owner = block(s, slot) // per_head
        if owner % 2 != h % 2:
            return 0
        return 1 if owner == h else 2

    groups = []
    for slots, chosen in wanted:
        clash = any(
            [role(s, h, slot) for slot in slots].count(r) > 1 for s in range(n) for h in range(heads) for r in (1, 2)
        )
        groups += [((slot,), chosen) for slot in slots] if clash else [(slots, chosen)]
    places, rows = [], [[] for _ in range(n * heads)]
    for slots, chosen in groups:
        places.append(len(rows[0]))
        for s in range(n):
            for h in range(heads):
                roles = [role(s, h, slot) for slot in slots]
                mine = [slot for slot, r in zip(slots, roles) if r == 1]
                column = block(s, mine[0]) % per_head if mine else 0
                if len(chosen) < pieces:
                    column = column * pieces + chosen[0]
                rows[s * heads + h] += [int(bool(mine)), column] + roles
    return ring, groups, places, rows, block


def solution(mesh):
    n, heads = mesh.shape["seq"], mesh.shape["head"]
    pairs = heads // 2
    per_head = n // heads
    half = n // 2

    def shards(queries, key_rows, value_rows, gate_logits, norm_gain, out_weight, doc_lengths):
        rows, width = queries.shape
        heads_here = width // HS
        columns = out_weight.shape[1]
        pieces = 2 if columns % 256 == 0 else 1
        part = columns // pieces
        ring, groups, places, table_rows, block = plan(n, heads, pieces)
        device = lax.axis_index("seq") * heads + lax.axis_index("head")
        table = lax.dynamic_index_in_dim(jnp.asarray(table_rows, jnp.int32), device, 0, keepdims=False)
        smem = pl.BlockSpec(memory_space=pltpu.SMEM)
        anywhere = pl.BlockSpec(memory_space=pl.ANY)
        head_block = pl.BlockSpec((rows, HS), lambda h: (0, h))
        two_heads = pl.BlockSpec((rows, 2 * HS), lambda h: (0, h))
        state_block = pl.BlockSpec((1, HS, HS), lambda h: (h, 0, 0))

        def core_of(s, slot):
            return (block(s, slot) // per_head) % 2

        def call(kernel, name, **options):
            return pl.pallas_call(kernel, compiler_params=params(), name=name, **options)

        summary = call(
            summary_kernel,
            "summary",
            grid=(heads_here // 2,),
            in_specs=[smem, two_heads, two_heads],
            out_specs=pl.BlockSpec((2, HS, HS), lambda h: (h, 0, 0)),
            out_shape=jax.ShapeDtypeStruct((heads_here, HS, HS), BF16),
            cost_estimate=cost(2 * rows * width * HS, 4 * rows * width),
        )(doc_lengths, key_rows, value_rows)

        def along(slot, step):
            target = {s: block(s, -step) for s in range(n)}
            return [
                (s * heads + 2 * y + core_of(s, slot), target[s] * heads + 2 * y + core_of(s, slot))
                for s in range(n)
                for y in range(pairs)
            ]

        gather = [
            (s * heads + 2 * y + 1 - core_of(s, 0), s * heads + 2 * y + core_of(s, 0))
            for s in range(n)
            for y in range(pairs)
        ]
        arrived = {}

        def send_on(k, i, *before):
            steps = (-1, 1) if k < half else (-1 if i % 2 == 0 else 1,)
            for step in steps:
                source = step * (k - 1)
                here = arrived.get((source, None), arrived.get((source, i)))
                if i is None or here.shape[0] == 1:
                    here = tie(here, *before)
                if i is not None and here.shape[0] > 1:
                    if (source, i) not in arrived:
                        both = [tie(arrived[x, None], *before) for x in (-source, source)]
                        split = call(
                            split_kernel,
                            "split",
                            out_shape=[jax.ShapeDtypeStruct((1, *here.shape[1:]), BF16)] * (2 * len(both)),
                            cost_estimate=cost(width * columns, 16 * width * columns),
                        )(*both)
                        for x, halves in zip((-source, source), (split[:2], split[2:])):
                            for j in range(2):
                                arrived[x, j] = halves[j]
                    here = arrived[source, i]
                arrived[half if k == half else step * k, i] = lax.ppermute(here, BOTH, along(source, step))

        def there(k, i):
            return [arrived[key] for key in ((-k, i), (k, i)) if key in arrived]

        gathered = lax.ppermute(out_weight, BOTH, gather)
        merged = call(
            merge_kernel,
            "merge",
            out_shape=jax.ShapeDtypeStruct((pieces, 2 * width, part), BF16),
            cost_estimate=cost(width * part, 8 * width * columns),
        )(out_weight, tie(gathered, summary))
        arrived[0, None] = merged

        other_state = lax.ppermute(summary, "seq", [(s, s ^ 1) for s in range(n)])
        send_on(1, None, other_state)

        def intra_of(first, count, *before):
            block_at = pl.BlockSpec((rows, HS), lambda h: (0, first + h))
            return call(
                functools.partial(intra_kernel, tile=256),
                "intra",
                grid=(count,),
                in_specs=[smem, block_at, block_at, block_at],
                out_specs=head_block,
                out_shape=jax.ShapeDtypeStruct((rows, count * HS), F32),
                scratch_shapes=[pltpu.VMEM((rows, HS), jnp.int32)],
                cost_estimate=cost(4 * rows * rows * count * HS, 10 * rows * count * HS),
            )(tie(doc_lengths, *before), queries, key_rows, value_rows)

        count = heads_here // 2
        whole_state = pl.BlockSpec((heads_here, HS, HS), lambda: (0, 0, 0))
        pair_state = call(
            functools.partial(pair_kernel, rows=rows),
            "pair_state",
            in_specs=[smem, whole_state, whole_state],
            out_specs=whole_state,
            out_shape=jax.ShapeDtypeStruct((heads_here, HS, HS), BF16),
            cost_estimate=cost(heads_here * HS * HS, 6 * heads_here * HS * HS),
        )(doc_lengths, tie(summary, merged), other_state)
        earlier = [
            lax.ppermute(pair_state, "seq", [(s, s + 2 * d) for s in range(n - 2 * d)]) for d in range(1, n // 4 + 1)
        ]
        intra_low = intra_of(0, count, pair_state, table)
        intra_high = intra_of(count, count, intra_low)
        for k in range(2, min(3, half - 1)):
            send_on(k, None, intra_high, *earlier)

        low = pl.BlockSpec((rows, 2 * HS), lambda h: (0, jnp.minimum(h, count // 2 - 1)))
        high = pl.BlockSpec((rows, 2 * HS), lambda h: (0, jnp.maximum(h - count // 2, 0)))
        two_states = pl.BlockSpec((2, HS, HS), lambda h: (h, 0, 0))
        head_out = call(
            functools.partial(finish_kernel, rows=rows, heads_low=count // 2),
            "finish",
            grid=(heads_here // 2,),
            in_specs=[smem, two_heads, low, high, two_heads, pl.BlockSpec((1, 2 * HS), lambda h: (0, h)), two_states]
            + [two_states] * len(earlier),
            out_specs=two_heads,
            out_shape=jax.ShapeDtypeStruct((rows, width), BF16),
            scratch_shapes=[pltpu.SMEM((2,), jnp.int32)],
            cost_estimate=cost(2 * rows * width * HS, 12 * rows * width),
        )(
            doc_lengths,
            queries,
            intra_low,
            intra_high,
            gate_logits,
            norm_gain.reshape(1, width),
            other_state,
            *earlier,
        )
        head_other = lax.ppermute(head_out, "head", [(h, h ^ 1) for h in range(heads)])

        tile = min(rows, 512)
        by_columns = part % 128 == 0
        out = []
        out_dims = (rows, per_head * columns) if by_columns else (per_head, rows, columns)
        row_tile = pl.BlockSpec((tile, width), lambda i: (i, 0))

        def share(g, *before):
            (slots, chosen), at = groups[g], places[g]
            wide = part * len(chosen)
            weights = [arrived[slot, None if (slot, None) in arrived else chosen[0]] for slot in slots]
            sent, kept = call(
                functools.partial(partial_kernel, slots=len(slots), at=at + 2),
                "partial",
                grid=(rows // tile,),
                in_specs=[smem, row_tile, row_tile] + [anywhere] * len(weights),
                out_specs=[pl.BlockSpec((tile, wide), lambda i: (i, 0))] * 2,
                out_shape=[jax.ShapeDtypeStruct((rows, wide), BF16), jax.ShapeDtypeStruct((rows, wide), F32)],
                scratch_shapes=[
                    pltpu.VMEM((len(slots), 2 * width, wide), BF16),
                    pltpu.SemaphoreType.DMA((len(slots), len(chosen))),
                ],
                cost_estimate=cost(4 * rows * width * wide, 4 * rows * width + 10 * rows * wide),
            )(tie(table, *before), head_out, head_other, *weights)
            received = []
            for d in range(1, pairs):
                to_owner = []
                for s in range(n):
                    for slot in slots:
                        y, core = divmod(block(s, slot) // per_head, 2)
                        to_owner.append((s * heads + 2 * ((y + d) % pairs) + core, s * heads + 2 * y + core))
                received.append(lax.ppermute(sent, BOTH, to_owner))
            return kept, received, sent

        def add(g, shares, *before):
            nonlocal out
            (slots, chosen), at = groups[g], places[g]
            kept, received, _ = shares
            wide = part * len(chosen)
            few = min(rows, 256)
            out = [
                call(
                    functools.partial(add_kernel, at=at, shares=len(received), tile=few),
                    "add_shares",
                    in_specs=[smem] + [anywhere] * (1 + len(received) + len(out)),
                    out_specs=anywhere,
                    out_shape=jax.ShapeDtypeStruct(out_dims, BF16),
                    input_output_aliases={2 + len(received): 0} if out else {},
                    scratch_shapes=[
                        pltpu.VMEM((rows, wide), F32),
                        pltpu.VMEM((len(received), rows, wide), BF16),
                        pltpu.VMEM((rows, wide), BF16),
                        pltpu.SemaphoreType.DMA((rows // few, 2 + len(received))),
                    ],
                    cost_estimate=cost(2 * rows * wide, 10 * rows * wide),
                )(tie(table, *before), kept, *received, *out)
            ]

        waiting, last = [], [head_out]
        near = [g for g, (slots, _) in enumerate(groups) if abs(slots[0]) == 1]
        order = near + [g for g in range(len(groups)) if g not in near]
        for g in order:
            slots, chosen = groups[g]
            k, i = abs(slots[0]), chosen[0]
            arrival = []
            if k == 2 and slots[0] < 0:
                if half > 4:
                    send_on(3, None, *last)
                else:
                    for j in range(pieces):
                        send_on(3, j, *last)
            elif 2 < k < half - 1 and slots[0] < 0:
                arrival = there(k, None)
                if k + 1 < half - 1:
                    send_on(k + 1, None, *last)
                else:
                    for j in range(pieces):
                        send_on(k + 1, j, *last)
            elif k == half - 1 and (half, i) not in arrived:
                send_on(half, i, *last)
            shares = share(g, *last, *arrival)
            waiting.append((g, shares))
            last = [shares[2]]
            if len(waiting) > 2:
                add(*waiting.pop(0), *last)
                last = out
        for g, pending in waiting:
            add(g, pending)
        out = out[0]
        if not by_columns:
            out = jnp.transpose(out, (1, 0, 2)).reshape(rows, per_head * columns)
        return out

    return jax.shard_map(
        shards,
        mesh=mesh,
        in_specs=(
            P("seq", "head"),
            P("seq", "head"),
            P("seq", "head"),
            P("seq", "head"),
            P("head"),
            P("head", "seq"),
            P(),
        ),
        out_specs=P("seq", "head"),
        check_vma=False,
    )
```

```python
import functools

import jax
import jax.numpy as jnp
from jax import lax
from jax.experimental import pallas as pl
from jax.experimental.pallas import tpu as pltpu
from jax.sharding import PartitionSpec as P

HS = 128
EPS = 1e-05
BOTH = ("seq", "head")
VMEM_LIMIT = 64 * 1024 * 1024
COST_SCALE = 4096
F32 = jnp.float32
BF16 = jnp.bfloat16


def params():
    return pltpu.CompilerParams(vmem_limit_bytes=VMEM_LIMIT)


def cost(flops, nbytes):
    return pl.CostEstimate(flops=flops // COST_SCALE, bytes_accessed=nbytes // COST_SCALE, transcendentals=0)


def tie(value, *before):
    return lax.optimization_barrier((value, *before))[0]


def doc_start_of(lengths_ref, position):
    def step(c, carry):
        start, found = carry
        found = jnp.where(start <= position, start, found)
        return start + lengths_ref[c], found

    _, found = lax.fori_loop(0, lengths_ref.shape[0], step, (jnp.int32(0), jnp.int32(0)))
    return found


def doc_start_rows(lengths_ref, first_pos, rows):
    positions = lax.broadcasted_iota(jnp.int32, (rows, HS), 0)
    found = jnp.full((rows, HS), -first_pos, jnp.int32)
    start = -first_pos
    for c in range(lengths_ref.shape[0]):
        found = jnp.where(start <= positions, start, found)
        start = start + lengths_ref[c]
    return found


def summary_kernel(lengths_ref, key_ref, value_ref, out_ref, scalar_ref):
    rows = key_ref.shape[0]
    first_pos = lax.axis_index("seq") * rows

    @pl.when(pl.program_id(0) == 0)
    def _():
        start, found = jnp.int32(0), jnp.int32(0)
        for c in range(lengths_ref.shape[0]):
            found = jnp.where(start <= first_pos + rows - 1, start, found)
            start = start + lengths_ref[c]
        scalar_ref[0] = found - first_pos

    last_start = scalar_ref[0]
    mask = lax.broadcasted_iota(jnp.int32, (rows, HS), 0) >= last_start
    for h in range(out_ref.shape[0]):
        at = slice(h * HS, (h + 1) * HS)
        keys = jnp.where(mask, key_ref[:, at].astype(F32), 0.0).astype(BF16)
        total = lax.dot_general(keys, value_ref[:, at], (((0,), (0,)), ((), ())), preferred_element_type=F32)
        out_ref[h] = total.astype(BF16)


def pair_kernel(lengths_ref, own_ref, other_ref, out_ref, *, rows):
    index = lax.axis_index("seq")
    odd = lax.rem(index, 2)
    odd_first = (index - odd + 1) * rows
    keep = (doc_start_of(lengths_ref, odd_first + rows - 1) < odd_first).astype(F32)
    own_scale = jnp.where(odd == 1, 1.0, keep)
    other_scale = jnp.where(odd == 1, keep, 1.0)
    out_ref[...] = (own_scale * own_ref[...].astype(F32) + other_scale * other_ref[...].astype(F32)).astype(BF16)


def intra_kernel(lengths_ref, query_ref, key_ref, value_ref, out_ref, start_ref, *, tile):
    rows = query_ref.shape[0]

    @pl.when(pl.program_id(0) == 0)
    def _():
        start_ref[...] = doc_start_rows(lengths_ref, lax.axis_index("seq") * rows, rows)

    for t in range(rows // tile):
        at = pl.ds(t * tile, tile)
        query = query_ref[at, :]
        starts = start_ref[at, 0:1]
        span = (t + 1) * tile
        scores = lax.dot_general(
            query, key_ref[pl.ds(0, span), :], (((1,), (1,)), ((), ())), preferred_element_type=F32
        )
        s = lax.broadcasted_iota(jnp.int32, (tile, span), 1)
        p = lax.broadcasted_iota(jnp.int32, (tile, span), 0) + t * tile
        weights = jnp.where((s <= p) & (s >= starts), scores, 0.0).astype(BF16)
        out_ref[at, :] = jnp.dot(weights, value_ref[pl.ds(0, span), :], preferred_element_type=F32)


def finish_kernel(
    lengths_ref, query_ref, low_ref, high_ref, gate_ref, gain_ref, other_ref, *rest, rows, heads_low
):
    pair_refs, (out_ref, scalars_ref) = rest[:-2], rest[-2:]
    index = lax.axis_index("seq")
    odd = lax.rem(index, 2)
    first_pos = index * rows
    pair_first = (index - odd) * rows

    @pl.when(pl.program_id(0) == 0)
    def _():
        start, before, end = jnp.int32(0), jnp.int32(0), jnp.int32(0)
        for c in range(lengths_ref.shape[0]):
            following = start + lengths_ref[c]
            inside = start <= first_pos - 1
            before = jnp.where(inside, start, before)
            end = jnp.where(inside, following, end)
            start = following
        scalars_ref[0] = before
        scalars_ref[1] = end

    before, end = scalars_ref[0], scalars_ref[1]
    inside = lax.broadcasted_iota(jnp.int32, (rows, HS), 0) < end - first_pos
    is_low = pl.program_id(0) < heads_low
    for h in range(other_ref.shape[0]):
        at = slice(h * HS, (h + 1) * HS)
        incoming = odd.astype(F32) * other_ref[h].astype(F32)
        for j, pair_ref in enumerate(pair_refs):
            live = (before < pair_first - j * 2 * rows).astype(F32)
            incoming = incoming + live * pair_ref[h].astype(F32)
        inter = jnp.dot(query_ref[:, at], incoming.astype(BF16), preferred_element_type=F32)
        intra = jnp.where(is_low, low_ref[:, at], high_ref[:, at])
        a = intra + jnp.where(inside, inter, 0.0)
        scale = lax.rsqrt(jnp.mean(a * a, axis=-1, keepdims=True) + EPS)
        gate = jax.nn.sigmoid(gate_ref[:, at].astype(F32))
        out_ref[:, at] = (a * scale * gain_ref[:, at] * gate).astype(BF16)


def merge_kernel(mine_ref, gathered_ref, out_ref):
    rows = mine_ref.shape[0]
    wide = out_ref.shape[2]
    for i in range(out_ref.shape[0]):
        out_ref[i, :rows, :] = mine_ref[:, i * wide : (i + 1) * wide]
        out_ref[i, rows:, :] = gathered_ref[:, i * wide : (i + 1) * wide]


def split_kernel(*refs):
    half = len(refs) // 3
    for i, ref in enumerate(refs[:half]):
        for j in range(2):
            refs[half + 2 * i + j][...] = ref[j : j + 1]


def partial_kernel(table_ref, own_ref, other_ref, *rest, slots, at):
    weights, (sent_ref, kept_ref, buffer_ref, sems) = rest[:slots], rest[slots:]
    pieces, _, columns = weights[0].shape

    def copies(slot):
        return [
            pltpu.make_async_copy(
                weights[slot].at[piece],
                buffer_ref.at[slot, :, pl.ds(piece * columns, columns)],
                sems.at[slot, piece],
            )
            for piece in range(pieces)
        ]

    @pl.when(pl.program_id(0) == 0)
    def _():
        for slot in range(slots):

            @pl.when(table_ref[at + slot] != 0)
            def _():
                for copy in copies(slot):
                    copy.start()

    for slot in range(slots):
        role = table_ref[at + slot]

        @pl.when((role != 0) & (pl.program_id(0) == 0))
        def _():
            for copy in copies(slot):
                copy.wait()

        @pl.when(role != 0)
        def _():
            features = jnp.concatenate([own_ref[...], other_ref[...]], axis=1)
            total = jnp.dot(features, buffer_ref[slot], preferred_element_type=F32)

            @pl.when(role == 1)
            def _():
                kept_ref[...] = total

            @pl.when(role == 2)
            def _():
                sent_ref[...] = total.astype(BF16)


def add_kernel(table_ref, kept_ref, *rest, at, shares, tile):
    received, (out_ref, kept_buffer, buffers, sum_buffer, sems) = rest[:shares], rest[-5:]
    rows, wide = kept_ref.shape
    tiles = rows // tile
    column = table_ref[at + 1]

    def copies_in(t):
        here = pl.ds(t * tile, tile)
        return [pltpu.make_async_copy(kept_ref.at[here, :], kept_buffer.at[here, :], sems.at[t, 0])] + [
            pltpu.make_async_copy(ref.at[here, :], buffers.at[i, here, :], sems.at[t, 1 + i])
            for i, ref in enumerate(received)
        ]

    def copy_out(t):
        here = pl.ds(t * tile, tile)
        if len(out_ref.shape) == 2:
            place = out_ref.at[here, pl.ds(pl.multiple_of(column * wide, 128), wide)]
        else:
            place = out_ref.at[column, here, :]
        return pltpu.make_async_copy(sum_buffer.at[here, :], place, sems.at[t, 1 + shares])

    @pl.when(table_ref[at] == 1)
    def _():
        for t in range(tiles):
            for copy in copies_in(t):
                copy.start()
        for t in range(tiles):
            for copy in copies_in(t):
                copy.wait()
            here = pl.ds(t * tile, tile)
            total = kept_buffer[here, :]
            for i in range(shares):
                total = total + buffers[i, here, :].astype(F32)
            sum_buffer[here, :] = total.astype(BF16)
            copy_out(t).start()
        for t in range(tiles):
            copy_out(t).wait()


def plan(n, heads, pieces):
    ring = list(range(0, n, 2)) + list(range(n - 1, 0, -2))
    spot = {s: p for p, s in enumerate(ring)}
    per_head = n // heads
    half = n // 2
    everything = tuple(range(pieces))
    wanted = [((0,), everything)]
    for k in range(1, half):
        if k < half - 1:
            wanted.append(((-k, k), everything))
        else:
            wanted += [((-k, k), (i,)) for i in everything]
    wanted += [((half,), (i,)) for i in everything]

    def block(s, slot):
        return ring[(spot[s] + slot) % n]

    def role(s, h, slot):
        owner = block(s, slot) // per_head
        if owner % 2 != h % 2:
            return 0
        return 1 if owner == h else 2

    groups = []
    for slots, chosen in wanted:
        clash = any(
            [role(s, h, slot) for slot in slots].count(r) > 1 for s in range(n) for h in range(heads) for r in (1, 2)
        )
        groups += [((slot,), chosen) for slot in slots] if clash else [(slots, chosen)]
    places, rows = [], [[] for _ in range(n * heads)]
    for slots, chosen in groups:
        places.append(len(rows[0]))
        for s in range(n):
            for h in range(heads):
                roles = [role(s, h, slot) for slot in slots]
                mine = [slot for slot, r in zip(slots, roles) if r == 1]
                column = block(s, mine[0]) % per_head if mine else 0
                if len(chosen) < pieces:
                    column = column * pieces + chosen[0]
                rows[s * heads + h] += [int(bool(mine)), column] + roles
    return ring, groups, places, rows, block


def solution(mesh):
    n, heads = mesh.shape["seq"], mesh.shape["head"]
    pairs = heads // 2
    per_head = n // heads
    half = n // 2

    def shards(queries, key_rows, value_rows, gate_logits, norm_gain, out_weight, doc_lengths):
        rows, width = queries.shape
        heads_here = width // HS
        columns = out_weight.shape[1]
        pieces = 2 if columns % 256 == 0 else 1
        part = columns // pieces
        ring, groups, places, table_rows, block = plan(n, heads, pieces)
        device = lax.axis_index("seq") * heads + lax.axis_index("head")
        table = lax.dynamic_index_in_dim(jnp.asarray(table_rows, jnp.int32), device, 0, keepdims=False)
        smem = pl.BlockSpec(memory_space=pltpu.SMEM)
        anywhere = pl.BlockSpec(memory_space=pl.ANY)
        head_block = pl.BlockSpec((rows, HS), lambda h: (0, h))
        two_heads = pl.BlockSpec((rows, 2 * HS), lambda h: (0, h))
        state_block = pl.BlockSpec((1, HS, HS), lambda h: (h, 0, 0))

        def core_of(s, slot):
            return (block(s, slot) // per_head) % 2

        def call(kernel, name, **options):
            return pl.pallas_call(kernel, compiler_params=params(), name=name, **options)

        summary = call(
            summary_kernel,
            "summary",
            grid=(heads_here // 2,),
            in_specs=[smem, two_heads, two_heads],
            out_specs=pl.BlockSpec((2, HS, HS), lambda h: (h, 0, 0)),
            out_shape=jax.ShapeDtypeStruct((heads_here, HS, HS), BF16),
            scratch_shapes=[pltpu.SMEM((1,), jnp.int32)],
            cost_estimate=cost(2 * rows * width * HS, 4 * rows * width),
        )(doc_lengths, key_rows, value_rows)

        def along(slot, step):
            target = {s: block(s, -step) for s in range(n)}
            return [
                (s * heads + 2 * y + core_of(s, slot), target[s] * heads + 2 * y + core_of(s, slot))
                for s in range(n)
                for y in range(pairs)
            ]

        gather = [
            (s * heads + 2 * y + 1 - core_of(s, 0), s * heads + 2 * y + core_of(s, 0))
            for s in range(n)
            for y in range(pairs)
        ]
        arrived = {}

        def send_on(k, i, *before):
            steps = (-1, 1) if k < half else (-1 if i % 2 == 0 else 1,)
            for step in steps:
                source = step * (k - 1)
                here = arrived.get((source, None), arrived.get((source, i)))
                if i is None or here.shape[0] == 1:
                    here = tie(here, *before)
                if i is not None and here.shape[0] > 1:
                    if (source, i) not in arrived:
                        both = [tie(arrived[x, None], *before) for x in (-source, source)]
                        split = call(
                            split_kernel,
                            "split",
                            out_shape=[jax.ShapeDtypeStruct((1, *here.shape[1:]), BF16)] * (2 * len(both)),
                            cost_estimate=cost(width * columns, 16 * width * columns),
                        )(*both)
                        for x, halves in zip((-source, source), (split[:2], split[2:])):
                            for j in range(2):
                                arrived[x, j] = halves[j]
                    here = arrived[source, i]
                arrived[half if k == half else step * k, i] = lax.ppermute(here, BOTH, along(source, step))

        def there(k, i):
            return [arrived[key] for key in ((-k, i), (k, i)) if key in arrived]

        gathered = lax.ppermute(out_weight, BOTH, gather)
        merged = call(
            merge_kernel,
            "merge",
            out_shape=jax.ShapeDtypeStruct((pieces, 2 * width, part), BF16),
            cost_estimate=cost(width * part, 8 * width * columns),
        )(out_weight, tie(gathered, summary))
        arrived[0, None] = merged

        other_state = lax.ppermute(summary, "seq", [(s, s ^ 1) for s in range(n)])
        send_on(1, None, other_state)

        def intra_of(first, count, *before):
            block_at = pl.BlockSpec((rows, HS), lambda h: (0, first + h))
            return call(
                functools.partial(intra_kernel, tile=256),
                "intra",
                grid=(count,),
                in_specs=[smem, block_at, block_at, block_at],
                out_specs=head_block,
                out_shape=jax.ShapeDtypeStruct((rows, count * HS), F32),
                scratch_shapes=[pltpu.VMEM((rows, HS), jnp.int32)],
                cost_estimate=cost(4 * rows * rows * count * HS, 10 * rows * count * HS),
            )(tie(doc_lengths, *before), queries, key_rows, value_rows)

        count = heads_here // 2
        whole_state = pl.BlockSpec((heads_here, HS, HS), lambda: (0, 0, 0))
        pair_state = call(
            functools.partial(pair_kernel, rows=rows),
            "pair_state",
            in_specs=[smem, whole_state, whole_state],
            out_specs=whole_state,
            out_shape=jax.ShapeDtypeStruct((heads_here, HS, HS), BF16),
            cost_estimate=cost(heads_here * HS * HS, 6 * heads_here * HS * HS),
        )(doc_lengths, tie(summary, merged), other_state)
        earlier = [
            lax.ppermute(pair_state, "seq", [(s, s + 2 * d) for s in range(n - 2 * d)]) for d in range(1, n // 4 + 1)
        ]
        intra_low = intra_of(0, count, pair_state, table)
        intra_high = intra_of(count, count, intra_low)
        for k in range(2, min(3, half - 1)):
            send_on(k, None, intra_high, *earlier)

        low = pl.BlockSpec((rows, 2 * HS), lambda h: (0, jnp.minimum(h, count // 2 - 1)))
        high = pl.BlockSpec((rows, 2 * HS), lambda h: (0, jnp.maximum(h - count // 2, 0)))
        two_states = pl.BlockSpec((2, HS, HS), lambda h: (h, 0, 0))
        head_out = call(
            functools.partial(finish_kernel, rows=rows, heads_low=count // 2),
            "finish",
            grid=(heads_here // 2,),
            in_specs=[smem, two_heads, low, high, two_heads, pl.BlockSpec((1, 2 * HS), lambda h: (0, h)), two_states]
            + [two_states] * len(earlier),
            out_specs=two_heads,
            out_shape=jax.ShapeDtypeStruct((rows, width), BF16),
            scratch_shapes=[pltpu.SMEM((2,), jnp.int32)],
            cost_estimate=cost(2 * rows * width * HS, 12 * rows * width),
        )(
            doc_lengths,
            queries,
            intra_low,
            intra_high,
            gate_logits,
            norm_gain.reshape(1, width),
            other_state,
            *earlier,
        )
        head_other = lax.ppermute(head_out, "head", [(h, h ^ 1) for h in range(heads)])

        tile = min(rows, 512)
        by_columns = part % 128 == 0
        out = []
        out_dims = (rows, per_head * columns) if by_columns else (per_head, rows, columns)
        row_tile = pl.BlockSpec((tile, width), lambda i: (i, 0))

        def share(g, *before):
            (slots, chosen), at = groups[g], places[g]
            wide = part * len(chosen)
            weights = [arrived[slot, None if (slot, None) in arrived else chosen[0]] for slot in slots]
            sent, kept = call(
                functools.partial(partial_kernel, slots=len(slots), at=at + 2),
                "partial",
                grid=(rows // tile,),
                in_specs=[smem, row_tile, row_tile] + [anywhere] * len(weights),
                out_specs=[pl.BlockSpec((tile, wide), lambda i: (i, 0))] * 2,
                out_shape=[jax.ShapeDtypeStruct((rows, wide), BF16), jax.ShapeDtypeStruct((rows, wide), F32)],
                scratch_shapes=[
                    pltpu.VMEM((len(slots), 2 * width, wide), BF16),
                    pltpu.SemaphoreType.DMA((len(slots), len(chosen))),
                ],
                cost_estimate=cost(4 * rows * width * wide, 4 * rows * width + 10 * rows * wide),
            )(tie(table, *before), head_out, head_other, *weights)
            received = []
            for d in range(1, pairs):
                to_owner = []
                for s in range(n):
                    for slot in slots:
                        y, core = divmod(block(s, slot) // per_head, 2)
                        to_owner.append((s * heads + 2 * ((y + d) % pairs) + core, s * heads + 2 * y + core))
                received.append(lax.ppermute(sent, BOTH, to_owner))
            return kept, received, sent

        def add(g, shares, *before):
            nonlocal out
            (slots, chosen), at = groups[g], places[g]
            kept, received, _ = shares
            wide = part * len(chosen)
            few = min(rows, 256)
            out = [
                call(
                    functools.partial(add_kernel, at=at, shares=len(received), tile=few),
                    "add_shares",
                    in_specs=[smem] + [anywhere] * (1 + len(received) + len(out)),
                    out_specs=anywhere,
                    out_shape=jax.ShapeDtypeStruct(out_dims, BF16),
                    input_output_aliases={2 + len(received): 0} if out else {},
                    scratch_shapes=[
                        pltpu.VMEM((rows, wide), F32),
                        pltpu.VMEM((len(received), rows, wide), BF16),
                        pltpu.VMEM((rows, wide), BF16),
                        pltpu.SemaphoreType.DMA((rows // few, 2 + len(received))),
                    ],
                    cost_estimate=cost(2 * rows * wide, 10 * rows * wide),
                )(tie(table, *before), kept, *received, *out)
            ]

        waiting, last = [], [head_out]
        near = [g for g, (slots, _) in enumerate(groups) if abs(slots[0]) == 1]
        order = near + [g for g in range(len(groups)) if g not in near]
        for g in order:
            slots, chosen = groups[g]
            k, i = abs(slots[0]), chosen[0]
            arrival = []
            if k == 2 and slots[0] < 0:
                if half > 4:
                    send_on(3, None, *last)
                else:
                    for j in range(pieces):
                        send_on(3, j, *last)
            elif 2 < k < half - 1 and slots[0] < 0:
                arrival = there(k, None)
                if k + 1 < half - 1:
                    send_on(k + 1, None, *last)
                else:
                    for j in range(pieces):
                        send_on(k + 1, j, *last)
            elif k == half - 1 and (half, i) not in arrived:
                send_on(half, i, *last)
            shares = share(g, *last, *arrival)
            waiting.append((g, shares))
            last = [shares[2]]
            if len(waiting) > 2:
                add(*waiting.pop(0), *last)
                last = out
        for g, pending in waiting:
            add(g, pending)
        out = out[0]
        if not by_columns:
            out = jnp.transpose(out, (1, 0, 2)).reshape(rows, per_head * columns)
        return out

    return jax.shard_map(
        shards,
        mesh=mesh,
        in_specs=(
            P("seq", "head"),
            P("seq", "head"),
            P("seq", "head"),
            P("seq", "head"),
            P("head"),
            P("head", "seq"),
            P(),
        ),
        out_specs=P("seq", "head"),
        check_vma=False,
    )
```

```python
import functools

import jax
import jax.numpy as jnp
from jax import lax
from jax.experimental import pallas as pl
from jax.experimental.pallas import tpu as pltpu
from jax.sharding import PartitionSpec as P

HS = 128
EPS = 1e-05
BOTH = ("seq", "head")
VMEM_LIMIT = 64 * 1024 * 1024
COST_SCALE = 4096
F32 = jnp.float32
BF16 = jnp.bfloat16


def params():
    return pltpu.CompilerParams(vmem_limit_bytes=VMEM_LIMIT)


def cost(flops, nbytes):
    return pl.CostEstimate(flops=flops // COST_SCALE, bytes_accessed=nbytes // COST_SCALE, transcendentals=0)


def tie(value, *before):
    return lax.optimization_barrier((value, *before))[0]


def doc_start_of(lengths_ref, position):
    def step(c, carry):
        start, found = carry
        found = jnp.where(start <= position, start, found)
        return start + lengths_ref[c], found

    _, found = lax.fori_loop(0, lengths_ref.shape[0], step, (jnp.int32(0), jnp.int32(0)))
    return found


def doc_start_rows(lengths_ref, first_pos, rows):
    positions = lax.broadcasted_iota(jnp.int32, (rows, HS), 0)
    found = jnp.full((rows, HS), -first_pos, jnp.int32)
    start = -first_pos
    for c in range(lengths_ref.shape[0]):
        found = jnp.where(start <= positions, start, found)
        start = start + lengths_ref[c]
    return found


def summary_kernel(lengths_ref, key_ref, value_ref, out_ref, scalar_ref):
    rows = key_ref.shape[0]
    first_pos = lax.axis_index("seq") * rows

    @pl.when(pl.program_id(0) == 0)
    def _():
        start, found = jnp.int32(0), jnp.int32(0)
        for c in range(lengths_ref.shape[0]):
            found = jnp.where(start <= first_pos + rows - 1, start, found)
            start = start + lengths_ref[c]
        scalar_ref[0] = found - first_pos

    last_start = scalar_ref[0]
    mask = lax.broadcasted_iota(jnp.int32, (rows, HS), 0) >= last_start
    for h in range(out_ref.shape[0]):
        at = slice(h * HS, (h + 1) * HS)
        keys = jnp.where(mask, key_ref[:, at].astype(F32), 0.0).astype(BF16)
        total = lax.dot_general(keys, value_ref[:, at], (((0,), (0,)), ((), ())), preferred_element_type=F32)
        out_ref[h] = total.astype(BF16)


def pair_kernel(lengths_ref, own_ref, other_ref, out_ref, *, rows):
    index = lax.axis_index("seq")
    odd = lax.rem(index, 2)
    odd_first = (index - odd + 1) * rows
    keep = (doc_start_of(lengths_ref, odd_first + rows - 1) < odd_first).astype(F32)
    own_scale = jnp.where(odd == 1, 1.0, keep)
    other_scale = jnp.where(odd == 1, keep, 1.0)
    out_ref[...] = (own_scale * own_ref[...].astype(F32) + other_scale * other_ref[...].astype(F32)).astype(BF16)


def intra_kernel(lengths_ref, query_ref, key_ref, value_ref, out_ref, start_ref, *, tile):
    rows = query_ref.shape[0]

    @pl.when(pl.program_id(0) == 0)
    def _():
        start_ref[...] = doc_start_rows(lengths_ref, lax.axis_index("seq") * rows, rows)

    for t in range(rows // tile):
        at = pl.ds(t * tile, tile)
        query = query_ref[at, :]
        starts = start_ref[at, 0:1]
        span = (t + 1) * tile
        scores = lax.dot_general(
            query, key_ref[pl.ds(0, span), :], (((1,), (1,)), ((), ())), preferred_element_type=F32
        )
        s = lax.broadcasted_iota(jnp.int32, (tile, span), 1)
        p = lax.broadcasted_iota(jnp.int32, (tile, span), 0) + t * tile
        weights = jnp.where((s <= p) & (s >= starts), scores, 0.0).astype(BF16)
        out_ref[at, :] = jnp.dot(weights, value_ref[pl.ds(0, span), :], preferred_element_type=F32)


def finish_kernel(
    lengths_ref, query_ref, low_ref, high_ref, gate_ref, gain_ref, other_ref, *rest, rows, heads_low
):
    pair_refs, (out_ref, scalars_ref) = rest[:-2], rest[-2:]
    index = lax.axis_index("seq")
    odd = lax.rem(index, 2)
    first_pos = index * rows
    pair_first = (index - odd) * rows

    @pl.when(pl.program_id(0) == 0)
    def _():
        start, before, end = jnp.int32(0), jnp.int32(0), jnp.int32(0)
        for c in range(lengths_ref.shape[0]):
            following = start + lengths_ref[c]
            inside = start <= first_pos - 1
            before = jnp.where(inside, start, before)
            end = jnp.where(inside, following, end)
            start = following
        scalars_ref[0] = before
        scalars_ref[1] = end

    before, end = scalars_ref[0], scalars_ref[1]
    inside = lax.broadcasted_iota(jnp.int32, (rows, HS), 0) < end - first_pos
    is_low = pl.program_id(0) < heads_low
    for h in range(other_ref.shape[0]):
        at = slice(h * HS, (h + 1) * HS)
        incoming = odd.astype(F32) * other_ref[h].astype(F32)
        for j, pair_ref in enumerate(pair_refs):
            live = (before < pair_first - j * 2 * rows).astype(F32)
            incoming = incoming + live * pair_ref[h].astype(F32)
        inter = jnp.dot(query_ref[:, at], incoming.astype(BF16), preferred_element_type=F32)
        intra = jnp.where(is_low, low_ref[:, at], high_ref[:, at])
        a = intra + jnp.where(inside, inter, 0.0)
        scale = lax.rsqrt(jnp.mean(a * a, axis=-1, keepdims=True) + EPS)
        gate = jax.nn.sigmoid(gate_ref[:, at].astype(F32))
        out_ref[:, at] = (a * scale * gain_ref[:, at] * gate).astype(BF16)


def merge_kernel(mine_ref, gathered_ref, out_ref):
    rows = mine_ref.shape[0]
    wide = out_ref.shape[2]
    for i in range(out_ref.shape[0]):
        out_ref[i, :rows, :] = mine_ref[:, i * wide : (i + 1) * wide]
        out_ref[i, rows:, :] = gathered_ref[:, i * wide : (i + 1) * wide]


def split_kernel(*refs):
    half = len(refs) // 3
    for i, ref in enumerate(refs[:half]):
        for j in range(2):
            refs[half + 2 * i + j][...] = ref[j : j + 1]


def partial_kernel(table_ref, own_ref, other_ref, *rest, slots, at):
    weights, (sent_ref, kept_ref, buffer_ref, sems) = rest[:slots], rest[slots:]
    pieces, _, columns = weights[0].shape

    def copies(slot):
        return [
            pltpu.make_async_copy(
                weights[slot].at[piece],
                buffer_ref.at[slot, :, pl.ds(piece * columns, columns)],
                sems.at[slot, piece],
            )
            for piece in range(pieces)
        ]

    @pl.when(pl.program_id(0) == 0)
    def _():
        for slot in range(slots):

            @pl.when(table_ref[at + slot] != 0)
            def _():
                for copy in copies(slot):
                    copy.start()

    for slot in range(slots):
        role = table_ref[at + slot]

        @pl.when((role != 0) & (pl.program_id(0) == 0))
        def _():
            for copy in copies(slot):
                copy.wait()

        @pl.when(role != 0)
        def _():
            features = jnp.concatenate([own_ref[...], other_ref[...]], axis=1)
            total = jnp.dot(features, buffer_ref[slot], preferred_element_type=F32)

            @pl.when(role == 1)
            def _():
                kept_ref[...] = total

            @pl.when(role == 2)
            def _():
                sent_ref[...] = total.astype(BF16)


def add_kernel(table_ref, kept_ref, *rest, at, shares, tile):
    received, (out_ref, kept_buffer, buffers, sum_buffer, sems) = rest[:shares], rest[-5:]
    rows, wide = kept_ref.shape
    tiles = rows // tile
    column = table_ref[at + 1]

    def copies_in(t):
        here = pl.ds(t * tile, tile)
        return [pltpu.make_async_copy(kept_ref.at[here, :], kept_buffer.at[here, :], sems.at[t, 0])] + [
            pltpu.make_async_copy(ref.at[here, :], buffers.at[i, here, :], sems.at[t, 1 + i])
            for i, ref in enumerate(received)
        ]

    def copy_out(t):
        here = pl.ds(t * tile, tile)
        if len(out_ref.shape) == 2:
            place = out_ref.at[here, pl.ds(pl.multiple_of(column * wide, 128), wide)]
        else:
            place = out_ref.at[column, here, :]
        return pltpu.make_async_copy(sum_buffer.at[here, :], place, sems.at[t, 1 + shares])

    @pl.when(table_ref[at] == 1)
    def _():
        for t in range(tiles):
            for copy in copies_in(t):
                copy.start()
        for t in range(tiles):
            for copy in copies_in(t):
                copy.wait()
            here = pl.ds(t * tile, tile)
            total = kept_buffer[here, :]
            for i in range(shares):
                total = total + buffers[i, here, :].astype(F32)
            sum_buffer[here, :] = total.astype(BF16)
            copy_out(t).start()
        for t in range(tiles):
            copy_out(t).wait()


def plan(n, heads, pieces):
    ring = list(range(0, n, 2)) + list(range(n - 1, 0, -2))
    spot = {s: p for p, s in enumerate(ring)}
    per_head = n // heads
    half = n // 2
    everything = tuple(range(pieces))
    wanted = [((0,), everything)]
    for k in range(1, half):
        if k < half - 1:
            wanted.append(((-k, k), everything))
        else:
            wanted += [((-k, k), (i,)) for i in everything]
    wanted += [((half,), (i,)) for i in everything]

    def block(s, slot):
        return ring[(spot[s] + slot) % n]

    def role(s, h, slot):
        owner = block(s, slot) // per_head
        if owner % 2 != h % 2:
            return 0
        return 1 if owner == h else 2

    groups = []
    for slots, chosen in wanted:
        clash = any(
            [role(s, h, slot) for slot in slots].count(r) > 1 for s in range(n) for h in range(heads) for r in (1, 2)
        )
        groups += [((slot,), chosen) for slot in slots] if clash else [(slots, chosen)]
    places, rows = [], [[] for _ in range(n * heads)]
    for slots, chosen in groups:
        places.append(len(rows[0]))
        for s in range(n):
            for h in range(heads):
                roles = [role(s, h, slot) for slot in slots]
                mine = [slot for slot, r in zip(slots, roles) if r == 1]
                column = block(s, mine[0]) % per_head if mine else 0
                if len(chosen) < pieces:
                    column = column * pieces + chosen[0]
                rows[s * heads + h] += [int(bool(mine)), column] + roles
    return ring, groups, places, rows, block


def solution(mesh):
    n, heads = mesh.shape["seq"], mesh.shape["head"]
    pairs = heads // 2
    per_head = n // heads
    half = n // 2

    def shards(queries, key_rows, value_rows, gate_logits, norm_gain, out_weight, doc_lengths):
        rows, width = queries.shape
        heads_here = width // HS
        columns = out_weight.shape[1]
        pieces = 2 if columns % 256 == 0 else 1
        part = columns // pieces
        ring, groups, places, table_rows, block = plan(n, heads, pieces)
        device = lax.axis_index("seq") * heads + lax.axis_index("head")
        table = lax.dynamic_index_in_dim(jnp.asarray(table_rows, jnp.int32), device, 0, keepdims=False)
        smem = pl.BlockSpec(memory_space=pltpu.SMEM)
        anywhere = pl.BlockSpec(memory_space=pl.ANY)
        head_block = pl.BlockSpec((rows, HS), lambda h: (0, h))
        two_heads = pl.BlockSpec((rows, 2 * HS), lambda h: (0, h))
        state_block = pl.BlockSpec((1, HS, HS), lambda h: (h, 0, 0))

        def core_of(s, slot):
            return (block(s, slot) // per_head) % 2

        def call(kernel, name, **options):
            return pl.pallas_call(kernel, compiler_params=params(), name=name, **options)

        summary = call(
            summary_kernel,
            "summary",
            grid=(heads_here // 4,),
            in_specs=[smem] + [pl.BlockSpec((rows, 4 * HS), lambda h: (0, h))] * 2,
            out_specs=pl.BlockSpec((4, HS, HS), lambda h: (h, 0, 0)),
            out_shape=jax.ShapeDtypeStruct((heads_here, HS, HS), BF16),
            scratch_shapes=[pltpu.SMEM((1,), jnp.int32)],
            cost_estimate=cost(2 * rows * width * HS, 4 * rows * width),
        )(doc_lengths, key_rows, value_rows)

        def along(slot, step):
            target = {s: block(s, -step) for s in range(n)}
            return [
                (s * heads + 2 * y + core_of(s, slot), target[s] * heads + 2 * y + core_of(s, slot))
                for s in range(n)
                for y in range(pairs)
            ]

        gather = [
            (s * heads + 2 * y + 1 - core_of(s, 0), s * heads + 2 * y + core_of(s, 0))
            for s in range(n)
            for y in range(pairs)
        ]
        arrived = {}

        def send_on(k, i, *before):
            steps = (-1, 1) if k < half else (-1 if i % 2 == 0 else 1,)
            for step in steps:
                source = step * (k - 1)
                here = arrived.get((source, None), arrived.get((source, i)))
                if i is None or here.shape[0] == 1:
                    here = tie(here, *before)
                if i is not None and here.shape[0] > 1:
                    if (source, i) not in arrived:
                        both = [tie(arrived[x, None], *before) for x in (-source, source)]
                        split = call(
                            split_kernel,
                            "split",
                            out_shape=[jax.ShapeDtypeStruct((1, *here.shape[1:]), BF16)] * (2 * len(both)),
                            cost_estimate=cost(width * columns, 16 * width * columns),
                        )(*both)
                        for x, halves in zip((-source, source), (split[:2], split[2:])):
                            for j in range(2):
                                arrived[x, j] = halves[j]
                    here = arrived[source, i]
                arrived[half if k == half else step * k, i] = lax.ppermute(here, BOTH, along(source, step))

        def there(k, i):
            return [arrived[key] for key in ((-k, i), (k, i)) if key in arrived]

        gathered = lax.ppermute(out_weight, BOTH, gather)
        merged = call(
            merge_kernel,
            "merge",
            out_shape=jax.ShapeDtypeStruct((pieces, 2 * width, part), BF16),
            cost_estimate=cost(width * part, 8 * width * columns),
        )(out_weight, tie(gathered, summary))
        arrived[0, None] = merged

        other_state = lax.ppermute(summary, "seq", [(s, s ^ 1) for s in range(n)])
        send_on(1, None, other_state)

        def intra_of(first, count, *before):
            block_at = pl.BlockSpec((rows, HS), lambda h: (0, first + h))
            return call(
                functools.partial(intra_kernel, tile=256),
                "intra",
                grid=(count,),
                in_specs=[smem, block_at, block_at, block_at],
                out_specs=head_block,
                out_shape=jax.ShapeDtypeStruct((rows, count * HS), F32),
                scratch_shapes=[pltpu.VMEM((rows, HS), jnp.int32)],
                cost_estimate=cost(4 * rows * rows * count * HS, 10 * rows * count * HS),
            )(tie(doc_lengths, *before), queries, key_rows, value_rows)

        count = heads_here // 2
        whole_state = pl.BlockSpec((heads_here, HS, HS), lambda: (0, 0, 0))
        pair_state = call(
            functools.partial(pair_kernel, rows=rows),
            "pair_state",
            in_specs=[smem, whole_state, whole_state],
            out_specs=whole_state,
            out_shape=jax.ShapeDtypeStruct((heads_here, HS, HS), BF16),
            cost_estimate=cost(heads_here * HS * HS, 6 * heads_here * HS * HS),
        )(doc_lengths, tie(summary, merged), other_state)
        earlier = [
            lax.ppermute(pair_state, "seq", [(s, s + 2 * d) for s in range(n - 2 * d)]) for d in range(1, n // 4 + 1)
        ]
        intra_low = intra_of(0, count, pair_state, table)
        intra_high = intra_of(count, count, intra_low)
        for k in range(2, min(3, half - 1)):
            send_on(k, None, intra_high, *earlier)

        low = pl.BlockSpec((rows, 2 * HS), lambda h: (0, jnp.minimum(h, count // 2 - 1)))
        high = pl.BlockSpec((rows, 2 * HS), lambda h: (0, jnp.maximum(h - count // 2, 0)))
        two_states = pl.BlockSpec((2, HS, HS), lambda h: (h, 0, 0))
        head_out = call(
            functools.partial(finish_kernel, rows=rows, heads_low=count // 2),
            "finish",
            grid=(heads_here // 2,),
            in_specs=[smem, two_heads, low, high, two_heads, pl.BlockSpec((1, 2 * HS), lambda h: (0, h)), two_states]
            + [two_states] * len(earlier),
            out_specs=two_heads,
            out_shape=jax.ShapeDtypeStruct((rows, width), BF16),
            scratch_shapes=[pltpu.SMEM((2,), jnp.int32)],
            cost_estimate=cost(2 * rows * width * HS, 12 * rows * width),
        )(
            doc_lengths,
            queries,
            intra_low,
            intra_high,
            gate_logits,
            norm_gain.reshape(1, width),
            other_state,
            *earlier,
        )
        head_other = lax.ppermute(head_out, "head", [(h, h ^ 1) for h in range(heads)])

        tile = min(rows, 512)
        by_columns = part % 128 == 0
        out = []
        out_dims = (rows, per_head * columns) if by_columns else (per_head, rows, columns)
        row_tile = pl.BlockSpec((tile, width), lambda i: (i, 0))

        def share(g, *before):
            (slots, chosen), at = groups[g], places[g]
            wide = part * len(chosen)
            weights = [arrived[slot, None if (slot, None) in arrived else chosen[0]] for slot in slots]
            sent, kept = call(
                functools.partial(partial_kernel, slots=len(slots), at=at + 2),
                "partial",
                grid=(rows // tile,),
                in_specs=[smem, row_tile, row_tile] + [anywhere] * len(weights),
                out_specs=[pl.BlockSpec((tile, wide), lambda i: (i, 0))] * 2,
                out_shape=[jax.ShapeDtypeStruct((rows, wide), BF16), jax.ShapeDtypeStruct((rows, wide), F32)],
                scratch_shapes=[
                    pltpu.VMEM((len(slots), 2 * width, wide), BF16),
                    pltpu.SemaphoreType.DMA((len(slots), len(chosen))),
                ],
                cost_estimate=cost(4 * rows * width * wide, 4 * rows * width + 10 * rows * wide),
            )(tie(table, *before), head_out, head_other, *weights)
            received = []
            for d in range(1, pairs):
                to_owner = []
                for s in range(n):
                    for slot in slots:
                        y, core = divmod(block(s, slot) // per_head, 2)
                        to_owner.append((s * heads + 2 * ((y + d) % pairs) + core, s * heads + 2 * y + core))
                received.append(lax.ppermute(sent, BOTH, to_owner))
            return kept, received, sent

        def add(g, shares, *before):
            nonlocal out
            (slots, chosen), at = groups[g], places[g]
            kept, received, _ = shares
            wide = part * len(chosen)
            few = min(rows, 256)
            out = [
                call(
                    functools.partial(add_kernel, at=at, shares=len(received), tile=few),
                    "add_shares",
                    in_specs=[smem] + [anywhere] * (1 + len(received) + len(out)),
                    out_specs=anywhere,
                    out_shape=jax.ShapeDtypeStruct(out_dims, BF16),
                    input_output_aliases={2 + len(received): 0} if out else {},
                    scratch_shapes=[
                        pltpu.VMEM((rows, wide), F32),
                        pltpu.VMEM((len(received), rows, wide), BF16),
                        pltpu.VMEM((rows, wide), BF16),
                        pltpu.SemaphoreType.DMA((rows // few, 2 + len(received))),
                    ],
                    cost_estimate=cost(2 * rows * wide, 10 * rows * wide),
                )(tie(table, *before), kept, *received, *out)
            ]

        waiting, last = [], [head_out]
        near = [g for g, (slots, _) in enumerate(groups) if abs(slots[0]) == 1]
        order = near + [g for g in range(len(groups)) if g not in near]
        for g in order:
            slots, chosen = groups[g]
            k, i = abs(slots[0]), chosen[0]
            arrival = []
            if k == 2 and slots[0] < 0:
                if half > 4:
                    send_on(3, None, *last)
                else:
                    for j in range(pieces):
                        send_on(3, j, *last)
            elif 2 < k < half - 1 and slots[0] < 0:
                arrival = there(k, None)
                if k + 1 < half - 1:
                    send_on(k + 1, None, *last)
                else:
                    for j in range(pieces):
                        send_on(k + 1, j, *last)
            elif k == half - 1 and (half, i) not in arrived:
                send_on(half, i, *last)
            shares = share(g, *last, *arrival)
            waiting.append((g, shares))
            last = [shares[2]]
            if len(waiting) > 2:
                add(*waiting.pop(0), *last)
                last = out
        for g, pending in waiting:
            add(g, pending)
        out = out[0]
        if not by_columns:
            out = jnp.transpose(out, (1, 0, 2)).reshape(rows, per_head * columns)
        return out

    return jax.shard_map(
        shards,
        mesh=mesh,
        in_specs=(
            P("seq", "head"),
            P("seq", "head"),
            P("seq", "head"),
            P("seq", "head"),
            P("head"),
            P("head", "seq"),
            P(),
        ),
        out_specs=P("seq", "head"),
        check_vma=False,
    )
```
